256 devices in a mesh: path: 64 (over y, z, core), fsdp: 4 (over x).
Axes of the slice: x: 4, y: 4, z: 8, core: 2. Of those that a mesh axis runs over, the one named last changes fastest.
Arguments:
- inputs: bfloat16 [112640, 1024], P(('path', 'fsdp')), may hold values from -6 to 6
- cotangent: bfloat16 [112640, 1024], P(('path', 'fsdp')), may hold values from -6 to 6
- master: bfloat16 [16, 2, 1024, 4096], P(None, None, 'path', 'fsdp'), may hold values from -4 to 4
- momentum: float32 [16, 2, 1024, 4096], P(None, None, 'path', 'fsdp'), may hold values from -2 to 2
- sharing: int32 [64, 1], replicated, may hold values from 0 to 15
- block_owner: int32 [64], replicated, may hold values from 0 to 63, each once
Outputs:
- new_state: float32 [16, 2, 1024, 4096], P(None, None, 'path', 'fsdp')
- path_modules: bfloat16 [64, 2, 1024, 4096], P('path', None, None, 'fsdp')
The draws below stay inside these ranges and needn't reach their ends.
Inputs may be any that keep to these rules, and one draw needn't show every extreme that they name: `sharing`: each path names one module, and every module is named by one or more paths. `block_owner`: a permutation of the path indices.
All inputs are finite; a program needn't handle non-finite values.
Results may differ from the reference program's by a relative error of at most 0.0034.
Values may be sent and summed in bfloat16 or wider, within the bound.
No kernel may reach another device: no remote copies, remote signals or barrier semaphores. Data moves between devices by JAX's collectives and lax.ppermute only.
A program may use at most 128 MiB of HBM per device.

```python
import math
import jax
import jax.numpy as jnp
from jax import lax

D = 1024
FF = 4096
MODULES = 16
TOK_PATH = 1760
TOKENS = 112640
N_PATH = 64


def steps_of(own_key, extent, shards, smallest, high):
    factor_of, own = 1.0, jax.random.fold_in(own_key, 6)
    for dim, shards_of in shards:
        heights = jnp.exp(jax.random.uniform(jax.random.fold_in(own, dim), (shards_of,), jnp.float32, smallest / len(shards), high / len(shards)))
        factor_of = factor_of * jnp.repeat(heights, extent[dim] // shards_of).reshape([-1 if axis == dim else 1 for axis in range(len(extent))])
    return factor_of


def choose_distinct(stream_key, rows, count, top, lift):
    ranking = jax.random.permutation(jax.random.fold_in(stream_key, 1), count)
    favour = ranking
    for power in range(3):
        favour = favour * favour // count
    favour = favour * lift // count
    tickets = jax.random.randint(jax.random.fold_in(stream_key, 2), (rows, count), 0, 4096) + favour
    holders = jax.random.permutation(jax.random.fold_in(stream_key, 3), rows)[jnp.arange(count) % rows]
    tickets = jnp.where(jnp.arange(rows)[:, None] == holders[None, :], 1 << 14, tickets)
    merit = tickets * count + jnp.arange(count)
    return lax.top_k(merit.astype(jnp.int32), top)[1].astype(jnp.int32)


def normal_values(rng, dims, scale, most, cuts=(), kind=jnp.bfloat16):
    level = steps_of(rng, dims, cuts, -0.22, 0.18) if cuts else 1.0
    entries = jax.random.normal(rng, dims, jnp.float32) * scale * level
    return jnp.minimum(jnp.maximum(entries, -most), most).astype(kind)


def setup_inputs(seed: int = 0) -> dict:
    streams_of = jax.random.split(jax.random.key(seed), 7)
    inputs = normal_values(streams_of[0], (TOKENS, D), 1.0, 6.0, ((0, 256),))
    cotangent = normal_values(streams_of[1], (TOKENS, D), 1.0, 6.0, ((0, 256),))
    master = normal_values(streams_of[2], (MODULES, 2, D, FF), 1.0, 4.0, ((2, 64), (3, 4)))
    momentum = normal_values(streams_of[3], (MODULES, 2, D, FF), 0.3, 2.0, ((2, 64), (3, 4)), jnp.float32)
    sharing = choose_distinct(streams_of[4], N_PATH, MODULES, 1, 1024)
    block_owner = jax.random.permutation(streams_of[5], N_PATH).astype(jnp.int32)
    return {"inputs": inputs, "cotangent": cotangent, "master": master, "momentum": momentum, "sharing": sharing, "block_owner": block_owner}


inner_rate = 10.0
outer_rate = 0.7
outer_decay = 0.9

def silu_slope(values):
    sig = jax.nn.sigmoid(values)
    return sig * (1.0 + values * (1.0 - sig))

def path_delta(tokens_path, grads_path, module):
    pre_act = jnp.dot(tokens_path, module[0], preferred_element_type=jnp.float32) * (1.0 / math.sqrt(D))
    activation = jax.nn.silu(pre_act).astype(jnp.bfloat16)
    back_grad = jnp.dot(grads_path, module[1], preferred_element_type=jnp.float32) * (1.0 / math.sqrt(FF))
    slope_grad = (back_grad * silu_slope(pre_act)).astype(jnp.bfloat16)
    step_rate = inner_rate / math.sqrt(TOK_PATH)
    grad_down = lax.dot_general(grads_path, activation, (((0,), (0,)), ((), ())), preferred_element_type=jnp.float32) * (1.0 / math.sqrt(FF))
    grad_up = lax.dot_general(tokens_path, slope_grad, (((0,), (0,)), ((), ())), preferred_element_type=jnp.float32) * (1.0 / math.sqrt(D))
    return jnp.stack([(grad_up * step_rate).astype(jnp.bfloat16), (grad_down * step_rate).astype(jnp.bfloat16)])

def reference(inputs, cotangent, master, momentum, sharing, block_owner):
    block_rows = D // N_PATH
    module_of = sharing[:, 0]

    def to_logical(stored):
        blocks = stored.reshape(MODULES, 2, N_PATH, block_rows, FF)
        return blocks[:, :, block_owner].reshape(MODULES, 2, D, FF)
    weights = to_logical(master)

    def add_path(totals, path_index):
        row_start = (path_index * TOK_PATH).astype(jnp.int32)
        tokens_path = lax.dynamic_slice_in_dim(inputs, row_start, TOK_PATH, 0)
        grads_path = lax.dynamic_slice_in_dim(cotangent, row_start, TOK_PATH, 0)
        chosen = module_of[path_index]
        deltas = path_delta(tokens_path, grads_path, weights[chosen])
        return (totals.at[chosen].add(deltas.astype(jnp.float32)), None)
    totals, _ = lax.scan(add_path, jnp.zeros((MODULES, 2, D, FF), jnp.float32), jnp.arange(N_PATH, dtype=jnp.int32))
    onehot = module_of[None, :] == jnp.arange(MODULES, dtype=jnp.int32)[:, None]
    counts = lax.optimization_barrier(jnp.sum(onehot, axis=1)).astype(jnp.float32)
    averaged = totals / counts[:, None, None, None]
    state_new = outer_decay * to_logical(momentum) + averaged
    updated = (weights.astype(jnp.float32) - outer_rate * (averaged + outer_decay * state_new)).astype(jnp.bfloat16)
    state_blocks = state_new.reshape(MODULES, 2, N_PATH, block_rows, FF)
    stored_state = jnp.zeros_like(state_blocks).at[:, :, block_owner].set(state_blocks)
    new_state = stored_state.reshape(MODULES, 2, D, FF)
    path_modules = updated[module_of]
    return (new_state, path_modules)
```

```python
import functools
import math

import jax
import jax.numpy as jnp
from jax import lax
from jax.experimental import pallas as pl
from jax.experimental.pallas import tpu as pltpu
from jax.sharding import PartitionSpec as P

inner_rate = 10.0
outer_rate = 0.7
outer_decay = 0.9

VMEM_LIMIT = 56 * 1024 * 1024
ANY = pl.BlockSpec(memory_space=pl.ANY)
SMEM = pl.BlockSpec(memory_space=pltpu.SMEM)
VMEM = pl.BlockSpec(memory_space=pltpu.VMEM)


def params():
    return pltpu.CompilerParams(vmem_limit_bytes=VMEM_LIMIT)


def cost(flops, moved):
    return pl.CostEstimate(flops=flops, bytes_accessed=moved, transcendentals=0)


def wait_bytes(ref, sem):
    pltpu.make_async_copy(ref, ref, sem).wait()


def f32_dot(left, right):
    return jnp.dot(left, right, preferred_element_type=jnp.float32)


def pick_kernel(module_of, stored, out, sem):
    @pl.loop(0, out.shape[0])
    def _(path):
        pltpu.make_async_copy(stored.at[module_of[path]], out.at[path], sem).start()

    wait_bytes(out, sem)


def pick(module_of, stored):
    paths = module_of.shape[0]
    shape = (paths,) + stored.shape[1:]
    return pl.pallas_call(
        pick_kernel,
        out_shape=jax.ShapeDtypeStruct(shape, stored.dtype),
        in_specs=[SMEM, VMEM],
        out_specs=ANY,
        scratch_shapes=[pltpu.SemaphoreType.DMA],
        compiler_params=params(),
        cost_estimate=cost(0, 2 * math.prod(shape)),
        name="pick",
    )(module_of, stored)


def load_logical(owner, arrived, half, weight, sem):
    rows = arrived.shape[2]

    @pl.loop(0, arrived.shape[0])
    def _(block):
        pltpu.make_async_copy(
            arrived.at[owner[block], half],
            weight.at[pl.ds(pl.multiple_of(block * rows, rows), rows)],
            sem,
        ).start()


def store_blocks(owner, delta, out, first, count, sem):
    rows = out.shape[1]

    @pl.loop(first, first + count)
    def _(block):
        pltpu.make_async_copy(
            delta.at[pl.ds(pl.multiple_of(block * rows, rows), rows)],
            out.at[owner[block]],
            sem,
        ).start()


def sigmoid(values):
    return 1.0 / (1.0 + jnp.exp(-values))


def delta_rows(owner, left, right, scale, rate, delta, out, sem, tile):
    rows = out.shape[1]

    @pl.loop(0, left.shape[0] // tile)
    def _(step):
        at = pl.ds(pl.multiple_of(step * tile, tile), tile)
        grad = f32_dot(left[at, :], right[...]) * scale
        delta[at, :] = (grad * rate).astype(jnp.bfloat16)
        store_blocks(owner, delta, out, step * (tile // rows), tile // rows, sem)

    wait_bytes(delta, sem)


def down_kernel(
    scales, tile, parts, owner, arrived, tokens, grads_t, out,
    up_weight, tok, grd, act, delta, sems,
):
    scale_in, scale_hid, rate = scales
    part = tokens.shape[0] // parts
    load_logical(owner, arrived, 0, up_weight, sems.at[0])
    copies = [
        pltpu.make_async_copy(
            tokens.at[pl.ds(i * part, part)], tok.at[pl.ds(i * part, part)], sems.at[1 + i]
        )
        for i in range(parts)
    ]
    for copy in copies:
        copy.start()
    grads_copy = pltpu.make_async_copy(grads_t, grd, sems.at[1 + parts])
    grads_copy.start()
    wait_bytes(up_weight, sems.at[0])
    for i, copy in enumerate(copies):
        copy.wait()

        @pl.loop(0, act.shape[1] // tile)
        def _(step):
            at = pl.ds(pl.multiple_of(step * tile, tile), tile)
            pre = f32_dot(tok[pl.ds(i * part, part), :], up_weight[:, at]) * scale_in
            act[pl.ds(i * part, part), at] = (pre * sigmoid(pre)).astype(jnp.bfloat16)

    grads_copy.wait()
    delta_rows(owner, grd, act, scale_hid, rate, delta, out, sems.at[2 + parts], tile)


def up_kernel(
    scales, tile, parts, owner, arrived, tokens, grads, tokens_t, earlier, out,
    up_weight, down_weight, tok, grd, tok_t, slope, delta, sems,
):
    scale_in, scale_hid, rate = scales
    part = tokens.shape[0] // parts
    load_logical(owner, arrived, 0, up_weight, sems.at[0])
    load_logical(owner, arrived, 1, down_weight, sems.at[1])
    copies = [
        pltpu.make_async_copy(tokens, tok, sems.at[2]),
        pltpu.make_async_copy(grads, grd, sems.at[3]),
        pltpu.make_async_copy(tokens_t, tok_t, sems.at[4]),
    ]
    for copy in copies:
        copy.start()
    wait_bytes(up_weight, sems.at[0])
    wait_bytes(down_weight, sems.at[1])
    for copy in copies:
        copy.wait()
    for i in range(parts):

        @pl.loop(0, slope.shape[1] // tile)
        def _(step):
            at = pl.ds(pl.multiple_of(step * tile, tile), tile)
            rows = pl.ds(i * part, part)
            pre = f32_dot(tok[rows, :], up_weight[:, at]) * scale_in
            back = f32_dot(grd[rows, :], down_weight[:, at]) * scale_hid
            sig = sigmoid(pre)
            slope[rows, at] = (back * (sig * (1.0 + pre * (1.0 - sig)))).astype(jnp.bfloat16)

    delta_rows(owner, tok_t, slope, scale_in, rate, delta, out, sems.at[5], tile)


def delta_down(scales, owner, arrived, tokens, grads_t):
    paths, _, rows, cols = arrived.shape
    count, width = tokens.shape
    bf16 = jnp.bfloat16
    return pl.pallas_call(
        functools.partial(down_kernel, scales, 256, 2),
        out_shape=jax.ShapeDtypeStruct((paths, rows, cols), bf16),
        in_specs=[SMEM, ANY, ANY, ANY],
        out_specs=ANY,
        scratch_shapes=[
            pltpu.VMEM((width, cols), bf16),
            pltpu.VMEM((count, width), bf16),
            pltpu.VMEM((width, count), bf16),
            pltpu.VMEM((count, cols), bf16),
            pltpu.VMEM((width, cols), bf16),
            pltpu.SemaphoreType.DMA((5,)),
        ],
        compiler_params=params(),
        cost_estimate=cost(4 * count * width * cols, 4 * (2 * count * width + 2 * width * cols)),
        name="delta_down",
    )(owner, arrived, tokens, grads_t)


def delta_up(scales, owner, arrived, tokens, grads, tokens_t, earlier):
    paths, _, rows, cols = arrived.shape
    count, width = tokens.shape
    bf16 = jnp.bfloat16
    return pl.pallas_call(
        functools.partial(up_kernel, scales, 256, 2),
        out_shape=jax.ShapeDtypeStruct((paths, rows, cols), bf16),
        in_specs=[SMEM, ANY, ANY, ANY, ANY, ANY],
        out_specs=ANY,
        scratch_shapes=[
            pltpu.VMEM((width, cols), bf16),
            pltpu.VMEM((width, cols), bf16),
            pltpu.VMEM((count, width), bf16),
            pltpu.VMEM((count, width), bf16),
            pltpu.VMEM((width, count), bf16),
            pltpu.VMEM((count, cols), bf16),
            pltpu.VMEM((width, cols), bf16),
            pltpu.SemaphoreType.DMA((6,)),
        ],
        compiler_params=params(),
        cost_estimate=cost(6 * count * width * cols, 4 * (3 * count * width + 3 * width * cols)),
        name="delta_up",
    )(owner, arrived, tokens, grads, tokens_t, earlier)


def outer_step(module_of, received, master, momentum, state, updated, total):
    modules = total.shape[0]
    paths = received.shape[0]
    total[...] = jnp.zeros_like(total)

    @pl.loop(0, paths)
    def _(path):
        total[module_of[path]] += received[path].astype(jnp.float32)

    @pl.loop(0, modules)
    def _(module):
        count = lax.fori_loop(
            0, paths, lambda p, n: n + (module_of[p] == module).astype(jnp.int32), 0
        )
        averaged = total[module] / jnp.full(total.shape[1:], count, jnp.int32).astype(jnp.float32)
        new = outer_decay * momentum[module] + averaged
        state[module] = new
        weights = master[module].astype(jnp.float32)
        updated[module] = (weights - outer_rate * (averaged + outer_decay * new)).astype(
            jnp.bfloat16
        )


def outer_kernel(
    half, module_of, received, master, momentum, *refs,
):
    refs = refs[2:] if half == 0 else refs
    new_state, sending, got, mas, mom, state, updated, total, sems = refs
    copies = [
        pltpu.make_async_copy(received, got, sems.at[0]),
        pltpu.make_async_copy(master.at[:, half], mas, sems.at[1]),
        pltpu.make_async_copy(momentum.at[:, half], mom, sems.at[2]),
    ]
    for copy in copies:
        copy.start()
    for copy in copies:
        copy.wait()
    outer_step(module_of, got, mas, mom, state, updated, total)

    @pl.loop(0, sending.shape[0])
    def _(path):
        pltpu.make_async_copy(
            updated.at[module_of[path]], sending.at[path, half], sems.at[3]
        ).start()

    store = pltpu.make_async_copy(state, new_state.at[:, half], sems.at[4])
    store.start()
    wait_bytes(got, sems.at[3])
    store.wait()


def outer(half, module_of, received, master, momentum, earlier):
    paths, rows, cols = received.shape
    modules = master.shape[0]
    f32, bf16 = jnp.float32, jnp.bfloat16
    operands = (module_of, received, master, momentum) + earlier
    return pl.pallas_call(
        functools.partial(outer_kernel, half),
        out_shape=(
            jax.ShapeDtypeStruct(momentum.shape, f32),
            jax.ShapeDtypeStruct((paths, 2, rows, cols), bf16),
        ),
        in_specs=[SMEM] + [ANY] * (len(operands) - 1),
        out_specs=(ANY, ANY),
        scratch_shapes=[
            pltpu.VMEM((paths, rows, cols), bf16),
            pltpu.VMEM((modules, rows, cols), bf16),
            pltpu.VMEM((modules, rows, cols), f32),
            pltpu.VMEM((modules, rows, cols), f32),
            pltpu.VMEM((modules, rows, cols), bf16),
            pltpu.VMEM((modules, rows, cols), f32),
            pltpu.SemaphoreType.DMA((5,)),
        ],
        input_output_aliases={4: 0, 5: 1} if earlier else {},
        compiler_params=params(),
        cost_estimate=cost(paths * rows * cols, 4 * paths * rows * cols),
        name="outer",
    )(*operands)


def home_kernel(owner, back, out, sem):
    @pl.loop(0, back.shape[0])
    def _(block):
        for half in range(2):
            pltpu.make_async_copy(
                back.at[owner[block], half], out.at[half, block], sem
            ).start()

    wait_bytes(out, sem)


def bring_home(owner, back):
    paths, halves, rows, cols = back.shape
    return pl.pallas_call(
        home_kernel,
        out_shape=jax.ShapeDtypeStruct((halves, paths, rows, cols), back.dtype),
        in_specs=[SMEM, ANY],
        out_specs=ANY,
        scratch_shapes=[pltpu.SemaphoreType.DMA],
        compiler_params=params(),
        cost_estimate=cost(0, 4 * paths * halves * rows * cols),
        name="bring_home",
    )(owner, back)


def exchange(blocks):
    return lax.all_to_all(blocks, "path", split_axis=0, concat_axis=0, tiled=True)


def shards(inputs, cotangent, master, momentum, sharing, block_owner):
    block_cols = master.shape[3]
    module_of = sharing[:, 0]
    grads_all = lax.all_gather(cotangent, "fsdp", axis=0, tiled=True)
    tokens_all = lax.all_gather(inputs, "fsdp", axis=0, tiled=True)
    tok_rows, model_width = tokens_all.shape
    hidden_units = block_cols * lax.axis_size("fsdp")
    scales = (
        1.0 / math.sqrt(model_width),
        1.0 / math.sqrt(hidden_units),
        inner_rate / math.sqrt(tok_rows),
    )
    arrived = exchange(pick(module_of, master))
    down = delta_down(scales, block_owner, arrived, tokens_all, grads_all.T)
    got_down = exchange(down)
    up = delta_up(scales, block_owner, arrived, tokens_all, grads_all, tokens_all.T, down)
    got_up = exchange(up)
    earlier = outer(1, module_of, got_down, master, momentum, ())
    new_state, sending = outer(0, module_of, got_up, master, momentum, tuple(earlier))
    own_module = bring_home(block_owner, exchange(sending))
    return (new_state, own_module.reshape(1, 2, model_width, block_cols))


def solution(mesh):
    placed = (
        P(("path", "fsdp"), None),
        P(("path", "fsdp"), None),
        P(None, None, "path", "fsdp"),
        P(None, None, "path", "fsdp"),
        P(),
        P(),
    )
    return jax.shard_map(
        shards,
        mesh=mesh,
        in_specs=placed,
        out_specs=(P(None, None, "path", "fsdp"), P("path", None, None, "fsdp")),
        check_vma=False,
    )
```

```python
import functools
import math

import jax
import jax.numpy as jnp
from jax import lax
from jax.experimental import pallas as pl
from jax.experimental.pallas import tpu as pltpu
from jax.sharding import PartitionSpec as P

inner_rate = 10.0
outer_rate = 0.7
outer_decay = 0.9

VMEM_LIMIT = 56 * 1024 * 1024
ANY = pl.BlockSpec(memory_space=pl.ANY)
SMEM = pl.BlockSpec(memory_space=pltpu.SMEM)
VMEM = pl.BlockSpec(memory_space=pltpu.VMEM)


def params():
    return pltpu.CompilerParams(vmem_limit_bytes=VMEM_LIMIT)


def cost(flops, moved):
    return pl.CostEstimate(flops=flops, bytes_accessed=moved, transcendentals=0)


def wait_bytes(ref, sem):
    pltpu.make_async_copy(ref, ref, sem).wait()


def f32_dot(left, right):
    return jnp.dot(left, right, preferred_element_type=jnp.float32)


def pick_kernel(module_of, stored, out, sem):
    @pl.loop(0, out.shape[0])
    def _(path):
        pltpu.make_async_copy(stored.at[module_of[path]], out.at[path], sem).start()

    wait_bytes(out, sem)


def pick(module_of, stored):
    paths = module_of.shape[0]
    shape = (paths,) + stored.shape[1:]
    return pl.pallas_call(
        pick_kernel,
        out_shape=jax.ShapeDtypeStruct(shape, stored.dtype),
        in_specs=[SMEM, VMEM],
        out_specs=ANY,
        scratch_shapes=[pltpu.SemaphoreType.DMA],
        compiler_params=params(),
        cost_estimate=cost(0, 2 * math.prod(shape)),
        name="pick",
    )(module_of, stored)


def load_logical(owner, arrived, half, weight, sem):
    rows = arrived.shape[2]

    @pl.loop(0, arrived.shape[0])
    def _(block):
        pltpu.make_async_copy(
            arrived.at[owner[block], half],
            weight.at[pl.ds(pl.multiple_of(block * rows, rows), rows)],
            sem,
        ).start()


def store_blocks(owner, delta, out, first, count, sem):
    rows = out.shape[1]

    @pl.loop(first, first + count)
    def _(block):
        pltpu.make_async_copy(
            delta.at[pl.ds(pl.multiple_of(block * rows, rows), rows)],
            out.at[owner[block]],
            sem,
        ).start()


def sigmoid(values):
    return 1.0 / (1.0 + jnp.exp(-values))


def delta_rows(owner, left, right, scale, rate, delta, out, sem, tile):
    rows = out.shape[1]

    @pl.loop(0, left.shape[0] // tile)
    def _(step):
        at = pl.ds(pl.multiple_of(step * tile, tile), tile)
        grad = f32_dot(left[at, :], right[...]) * scale
        delta[at, :] = (grad * rate).astype(jnp.bfloat16)
        store_blocks(owner, delta, out, step * (tile // rows), tile // rows, sem)

    wait_bytes(delta, sem)


def down_kernel(
    scales, tile, parts, owner, arrived, tokens, grads_t, out,
    up_weight, tok, grd, act, delta, sems,
):
    scale_in, scale_hid, rate = scales
    part = tokens.shape[0] // parts
    load_logical(owner, arrived, 0, up_weight, sems.at[0])
    copies = [
        pltpu.make_async_copy(
            tokens.at[pl.ds(i * part, part)], tok.at[pl.ds(i * part, part)], sems.at[1 + i]
        )
        for i in range(parts)
    ]
    for copy in copies:
        copy.start()
    grads_copy = pltpu.make_async_copy(grads_t, grd, sems.at[1 + parts])
    grads_copy.start()
    wait_bytes(up_weight, sems.at[0])
    for i, copy in enumerate(copies):
        copy.wait()

        @pl.loop(0, act.shape[1] // tile)
        def _(step):
            at = pl.ds(pl.multiple_of(step * tile, tile), tile)
            pre = f32_dot(tok[pl.ds(i * part, part), :], up_weight[:, at]) * scale_in
            act[pl.ds(i * part, part), at] = (pre * sigmoid(pre)).astype(jnp.bfloat16)

    grads_copy.wait()
    delta_rows(owner, grd, act, scale_hid, rate, delta, out, sems.at[2 + parts], tile)


def up_kernel(
    scales, tile, parts, owner, arrived, tokens, grads, tokens_t, earlier, out,
    up_weight, down_weight, tok, grd, tok_t, slope, delta, sems,
):
    scale_in, scale_hid, rate = scales
    part = tokens.shape[0] // parts
    load_logical(owner, arrived, 0, up_weight, sems.at[0])
    load_logical(owner, arrived, 1, down_weight, sems.at[1])
    copies = [
        pltpu.make_async_copy(tokens, tok, sems.at[2]),
        pltpu.make_async_copy(grads, grd, sems.at[3]),
        pltpu.make_async_copy(tokens_t, tok_t, sems.at[4]),
    ]
    for copy in copies:
        copy.start()
    wait_bytes(up_weight, sems.at[0])
    wait_bytes(down_weight, sems.at[1])
    for copy in copies:
        copy.wait()
    for i in range(parts):

        @pl.loop(0, slope.shape[1] // tile)
        def _(step):
            at = pl.ds(pl.multiple_of(step * tile, tile), tile)
            rows = pl.ds(i * part, part)
            pre = f32_dot(tok[rows, :], up_weight[:, at]) * scale_in
            back = f32_dot(grd[rows, :], down_weight[:, at]) * scale_hid
            sig = sigmoid(pre)
            slope[rows, at] = (back * (sig * (1.0 + pre * (1.0 - sig)))).astype(jnp.bfloat16)

    delta_rows(owner, tok_t, slope, scale_in, rate, delta, out, sems.at[5], tile)


def delta_down(scales, owner, arrived, tokens, grads_t):
    paths, _, rows, cols = arrived.shape
    count, width = tokens.shape
    bf16 = jnp.bfloat16
    return pl.pallas_call(
        functools.partial(down_kernel, scales, 256, 2),
        out_shape=jax.ShapeDtypeStruct((paths, rows, cols), bf16),
        in_specs=[SMEM, ANY, ANY, ANY],
        out_specs=ANY,
        scratch_shapes=[
            pltpu.VMEM((width, cols), bf16),
            pltpu.VMEM((count, width), bf16),
            pltpu.VMEM((width, count), bf16),
            pltpu.VMEM((count, cols), bf16),
            pltpu.VMEM((width, cols), bf16),
            pltpu.SemaphoreType.DMA((5,)),
        ],
        compiler_params=params(),
        cost_estimate=cost(4 * count * width * cols, 4 * (2 * count * width + 2 * width * cols)),
        name="delta_down",
    )(owner, arrived, tokens, grads_t)


def delta_up(scales, owner, arrived, tokens, grads, tokens_t, earlier):
    paths, _, rows, cols = arrived.shape
    count, width = tokens.shape
    bf16 = jnp.bfloat16
    return pl.pallas_call(
        functools.partial(up_kernel, scales, 256, 2),
        out_shape=jax.ShapeDtypeStruct((paths, rows, cols), bf16),
        in_specs=[SMEM, ANY, ANY, ANY, ANY, ANY],
        out_specs=ANY,
        scratch_shapes=[
            pltpu.VMEM((width, cols), bf16),
            pltpu.VMEM((width, cols), bf16),
            pltpu.VMEM((count, width), bf16),
            pltpu.VMEM((count, width), bf16),
            pltpu.VMEM((width, count), bf16),
            pltpu.VMEM((count, cols), bf16),
            pltpu.VMEM((width, cols), bf16),
            pltpu.SemaphoreType.DMA((6,)),
        ],
        compiler_params=params(),
        cost_estimate=cost(6 * count * width * cols, 4 * (3 * count * width + 3 * width * cols)),
        name="delta_up",
    )(owner, arrived, tokens, grads, tokens_t, earlier)


def outer_kernel(half, module_of, order, received, master, momentum, *refs):
    refs = refs[2:] if half == 0 else refs
    new_state, sending, got, mas, mom, state, updated, first, sems = refs
    modules, rows, cols = state.shape
    paths = got.shape[0]
    copies = [
        pltpu.make_async_copy(received, got, sems.at[0]),
        pltpu.make_async_copy(master.at[:, half], mas, sems.at[1]),
        pltpu.make_async_copy(momentum.at[:, half], mom, sems.at[2]),
    ]
    for copy in copies:
        copy.start()

    for module in range(modules + 1):
        first[module] = 0

    @pl.loop(0, paths)
    def _(path):
        first[module_of[path] + 1] += 1

    for module in range(modules):
        first[module + 1] += first[module]
    for copy in copies:
        copy.wait()

    @pl.loop(0, modules)
    def _(module):
        begin, end = first[module], first[module + 1]
        total = lax.fori_loop(
            begin,
            end,
            lambda i, acc: acc + got[order[i]].astype(jnp.float32),
            jnp.zeros((rows, cols), jnp.float32),
        )
        averaged = total / jnp.full((rows, cols), end - begin, jnp.int32).astype(jnp.float32)
        new = outer_decay * mom[module] + averaged
        state[module] = new
        pltpu.make_async_copy(state.at[module], new_state.at[module, half], sems.at[4]).start()
        weights = mas[module].astype(jnp.float32)
        updated[module] = (weights - outer_rate * (averaged + outer_decay * new)).astype(
            jnp.bfloat16
        )

        @pl.loop(begin, end)
        def _(i):
            pltpu.make_async_copy(
                updated.at[module], sending.at[order[i], half], sems.at[3]
            ).start()

    wait_bytes(got, sems.at[3])
    wait_bytes(state, sems.at[4])


def outer(half, module_of, order, received, master, momentum, earlier):
    paths, rows, cols = received.shape
    modules = master.shape[0]
    f32, bf16 = jnp.float32, jnp.bfloat16
    operands = (module_of, order, received, master, momentum) + earlier
    return pl.pallas_call(
        functools.partial(outer_kernel, half),
        out_shape=(
            jax.ShapeDtypeStruct(momentum.shape, f32),
            jax.ShapeDtypeStruct((paths, 2, rows, cols), bf16),
        ),
        in_specs=[SMEM, SMEM] + [ANY] * (len(operands) - 2),
        out_specs=(ANY, ANY),
        scratch_shapes=[
            pltpu.VMEM((paths, rows, cols), bf16),
            pltpu.VMEM((modules, rows, cols), bf16),
            pltpu.VMEM((modules, rows, cols), f32),
            pltpu.VMEM((modules, rows, cols), f32),
            pltpu.VMEM((modules, rows, cols), bf16),
            pltpu.SMEM((modules + 1,), jnp.int32),
            pltpu.SemaphoreType.DMA((5,)),
        ],
        input_output_aliases={5: 0, 6: 1} if earlier else {},
        compiler_params=params(),
        cost_estimate=cost(paths * rows * cols, 4 * paths * rows * cols),
        name="outer",
    )(*operands)


def home_kernel(groups, owner, back, out, buf, sems):
    halves, blocks = out.shape[:2]
    per = blocks // groups
    parts = [(half, pl.ds(g * per, per)) for half in range(halves) for g in range(groups)]
    for i, (half, part) in enumerate(parts):

        @pl.loop(0, per)
        def _(step):
            block = part.start + step
            pltpu.make_async_copy(
                back.at[owner[block], half], buf.at[half, block], sems.at[i]
            ).start()

    stores = []
    for i, (half, part) in enumerate(parts):
        wait_bytes(buf.at[half, part], sems.at[i])
        store = pltpu.make_async_copy(
            buf.at[half, part], out.at[half, part], sems.at[len(parts) + i]
        )
        store.start()
        stores.append(store)
    for store in stores:
        store.wait()


def bring_home(owner, back):
    paths, halves, rows, cols = back.shape
    shape = (halves, paths, rows, cols)
    groups = 4
    return pl.pallas_call(
        functools.partial(home_kernel, groups),
        out_shape=jax.ShapeDtypeStruct(shape, back.dtype),
        in_specs=[SMEM, ANY],
        out_specs=ANY,
        scratch_shapes=[
            pltpu.VMEM(shape, back.dtype),
            pltpu.SemaphoreType.DMA((2 * halves * groups,)),
        ],
        compiler_params=params(),
        cost_estimate=cost(0, 4 * paths * halves * rows * cols),
        name="bring_home",
    )(owner, back)


def exchange(blocks):
    return lax.all_to_all(blocks, "path", split_axis=0, concat_axis=0, tiled=True)


def shards(inputs, cotangent, master, momentum, sharing, block_owner):
    block_cols = master.shape[3]
    module_of = sharing[:, 0]
    order = jnp.argsort(module_of)
    grads_all = lax.all_gather(cotangent, "fsdp", axis=0, tiled=True)
    tokens_all = lax.all_gather(inputs, "fsdp", axis=0, tiled=True)
    tok_rows, model_width = tokens_all.shape
    hidden_units = block_cols * lax.axis_size("fsdp")
    scales = (
        1.0 / math.sqrt(model_width),
        1.0 / math.sqrt(hidden_units),
        inner_rate / math.sqrt(tok_rows),
    )
    arrived = exchange(pick(module_of, master))
    down = delta_down(scales, block_owner, arrived, tokens_all, grads_all.T)
    got_down = exchange(down)
    up = delta_up(scales, block_owner, arrived, tokens_all, grads_all, tokens_all.T, down)
    got_up = exchange(up)
    earlier = outer(1, module_of, order, got_down, master, momentum, ())
    new_state, sending = outer(0, module_of, order, got_up, master, momentum, tuple(earlier))
    own_module = bring_home(block_owner, exchange(sending))
    return (new_state, own_module.reshape(1, 2, model_width, block_cols))


def solution(mesh):
    placed = (
        P(("path", "fsdp"), None),
        P(("path", "fsdp"), None),
        P(None, None, "path", "fsdp"),
        P(None, None, "path", "fsdp"),
        P(),
        P(),
    )
    return jax.shard_map(
        shards,
        mesh=mesh,
        in_specs=placed,
        out_specs=(P(None, None, "path", "fsdp"), P("path", None, None, "fsdp")),
        check_vma=False,
    )
```

```python
import functools
import math

import jax
import jax.numpy as jnp
from jax import lax
from jax.experimental import pallas as pl
from jax.experimental.pallas import tpu as pltpu
from jax.sharding import PartitionSpec as P

inner_rate = 10.0
outer_rate = 0.7
outer_decay = 0.9

VMEM_LIMIT = 56 * 1024 * 1024
ANY = pl.BlockSpec(memory_space=pl.ANY)
SMEM = pl.BlockSpec(memory_space=pltpu.SMEM)
VMEM = pl.BlockSpec(memory_space=pltpu.VMEM)


def params():
    return pltpu.CompilerParams(vmem_limit_bytes=VMEM_LIMIT)


def cost(flops, moved):
    return pl.CostEstimate(flops=flops, bytes_accessed=moved, transcendentals=0)


def wait_bytes(ref, sem):
    pltpu.make_async_copy(ref, ref, sem).wait()


def f32_dot(left, right):
    return jnp.dot(left, right, preferred_element_type=jnp.float32)


def pick_kernel(module_of, stored, out, sem):
    @pl.loop(0, out.shape[0])
    def _(path):
        pltpu.make_async_copy(stored.at[module_of[path]], out.at[path], sem).start()

    wait_bytes(out, sem)


def pick(module_of, stored):
    paths = module_of.shape[0]
    shape = (paths,) + stored.shape[1:]
    return pl.pallas_call(
        pick_kernel,
        out_shape=jax.ShapeDtypeStruct(shape, stored.dtype),
        in_specs=[SMEM, VMEM],
        out_specs=ANY,
        scratch_shapes=[pltpu.SemaphoreType.DMA],
        compiler_params=params(),
        cost_estimate=cost(0, 2 * math.prod(shape)),
        name="pick",
    )(module_of, stored)


def load_logical(owner, arrived, half, weight, sem):
    rows = arrived.shape[2]

    @pl.loop(0, arrived.shape[0])
    def _(block):
        pltpu.make_async_copy(
            arrived.at[owner[block], half],
            weight.at[pl.ds(pl.multiple_of(block * rows, rows), rows)],
            sem,
        ).start()


def store_blocks(owner, delta, out, first, count, sem):
    rows = out.shape[1]

    @pl.loop(first, first + count)
    def _(block):
        pltpu.make_async_copy(
            delta.at[pl.ds(pl.multiple_of(block * rows, rows), rows)],
            out.at[owner[block]],
            sem,
        ).start()


def sigmoid(values):
    return 1.0 / (1.0 + jnp.exp(-values))


def delta_rows(owner, left, right, scale, rate, delta, out, sem, tile):
    rows = out.shape[1]

    @pl.loop(0, left.shape[0] // tile)
    def _(step):
        at = pl.ds(pl.multiple_of(step * tile, tile), tile)
        grad = f32_dot(left[at, :], right[...]) * scale
        delta[at, :] = (grad * rate).astype(jnp.bfloat16)
        store_blocks(owner, delta, out, step * (tile // rows), tile // rows, sem)

    wait_bytes(delta, sem)


def down_kernel(
    scales, tile, parts, owner, arrived, tokens, grads_t, out,
    up_weight, tok, grd, act, delta, sems,
):
    scale_in, scale_hid, rate = scales
    part = tokens.shape[0] // parts
    load_logical(owner, arrived, 0, up_weight, sems.at[0])
    copies = [
        pltpu.make_async_copy(
            tokens.at[pl.ds(i * part, part)], tok.at[pl.ds(i * part, part)], sems.at[1 + i]
        )
        for i in range(parts)
    ]
    for copy in copies:
        copy.start()
    grads_copy = pltpu.make_async_copy(grads_t, grd, sems.at[1 + parts])
    grads_copy.start()
    wait_bytes(up_weight, sems.at[0])
    for i, copy in enumerate(copies):
        copy.wait()

        @pl.loop(0, act.shape[1] // tile)
        def _(step):
            at = pl.ds(pl.multiple_of(step * tile, tile), tile)
            pre = f32_dot(tok[pl.ds(i * part, part), :], up_weight[:, at]) * scale_in
            act[pl.ds(i * part, part), at] = (pre * sigmoid(pre)).astype(jnp.bfloat16)

    grads_copy.wait()
    delta_rows(owner, grd, act, scale_hid, rate, delta, out, sems.at[2 + parts], tile)


def up_kernel(
    scales, tile, parts, owner, arrived, tokens, grads, tokens_t, earlier, out,
    up_weight, down_weight, tok, grd, tok_t, slope, delta, sems,
):
    scale_in, scale_hid, rate = scales
    part = tokens.shape[0] // parts
    load_logical(owner, arrived, 0, up_weight, sems.at[0])
    load_logical(owner, arrived, 1, down_weight, sems.at[1])
    copies = [
        pltpu.make_async_copy(tokens, tok, sems.at[2]),
        pltpu.make_async_copy(grads, grd, sems.at[3]),
        pltpu.make_async_copy(tokens_t, tok_t, sems.at[4]),
    ]
    for copy in copies:
        copy.start()
    wait_bytes(up_weight, sems.at[0])
    wait_bytes(down_weight, sems.at[1])
    for copy in copies:
        copy.wait()
    for i in range(parts):

        @pl.loop(0, slope.shape[1] // tile)
        def _(step):
            at = pl.ds(pl.multiple_of(step * tile, tile), tile)
            rows = pl.ds(i * part, part)
            pre = f32_dot(tok[rows, :], up_weight[:, at]) * scale_in
            back = f32_dot(grd[rows, :], down_weight[:, at]) * scale_hid
            sig = sigmoid(pre)
            slope[rows, at] = (back * (sig * (1.0 + pre * (1.0 - sig)))).astype(jnp.bfloat16)

    delta_rows(owner, tok_t, slope, scale_in, rate, delta, out, sems.at[5], tile)


def delta_down(scales, owner, arrived, tokens, grads_t):
    paths, _, rows, cols = arrived.shape
    count, width = tokens.shape
    bf16 = jnp.bfloat16
    return pl.pallas_call(
        functools.partial(down_kernel, scales, 512, 2),
        out_shape=jax.ShapeDtypeStruct((paths, rows, cols), bf16),
        in_specs=[SMEM, ANY, ANY, ANY],
        out_specs=ANY,
        scratch_shapes=[
            pltpu.VMEM((width, cols), bf16),
            pltpu.VMEM((count, width), bf16),
            pltpu.VMEM((width, count), bf16),
            pltpu.VMEM((count, cols), bf16),
            pltpu.VMEM((width, cols), bf16),
            pltpu.SemaphoreType.DMA((5,)),
        ],
        compiler_params=params(),
        cost_estimate=cost(4 * count * width * cols, 4 * (2 * count * width + 2 * width * cols)),
        name="delta_down",
    )(owner, arrived, tokens, grads_t)


def delta_up(scales, owner, arrived, tokens, grads, tokens_t, earlier):
    paths, _, rows, cols = arrived.shape
    count, width = tokens.shape
    bf16 = jnp.bfloat16
    return pl.pallas_call(
        functools.partial(up_kernel, scales, 512, 2),
        out_shape=jax.ShapeDtypeStruct((paths, rows, cols), bf16),
        in_specs=[SMEM, ANY, ANY, ANY, ANY, ANY],
        out_specs=ANY,
        scratch_shapes=[
            pltpu.VMEM((width, cols), bf16),
            pltpu.VMEM((width, cols), bf16),
            pltpu.VMEM((count, width), bf16),
            pltpu.VMEM((count, width), bf16),
            pltpu.VMEM((width, count), bf16),
            pltpu.VMEM((count, cols), bf16),
            pltpu.VMEM((width, cols), bf16),
            pltpu.SemaphoreType.DMA((6,)),
        ],
        compiler_params=params(),
        cost_estimate=cost(6 * count * width * cols, 4 * (3 * count * width + 3 * width * cols)),
        name="delta_up",
    )(owner, arrived, tokens, grads, tokens_t, earlier)


def outer_kernel(half, module_of, order, received, master, momentum, *refs):
    refs = refs[2:] if half == 0 else refs
    new_state, sending, got, mas, mom, state, updated, first, sems = refs
    modules, rows, cols = state.shape
    paths = got.shape[0]
    copies = [
        pltpu.make_async_copy(received, got, sems.at[0]),
        pltpu.make_async_copy(master.at[:, half], mas, sems.at[1]),
        pltpu.make_async_copy(momentum.at[:, half], mom, sems.at[2]),
    ]
    for copy in copies:
        copy.start()

    for module in range(modules + 1):
        first[module] = 0

    @pl.loop(0, paths)
    def _(path):
        first[module_of[path] + 1] += 1

    for module in range(modules):
        first[module + 1] += first[module]
    for copy in copies:
        copy.wait()

    @pl.loop(0, modules)
    def _(module):
        begin, end = first[module], first[module + 1]
        total = lax.fori_loop(
            begin,
            end,
            lambda i, acc: acc + got[order[i]].astype(jnp.float32),
            jnp.zeros((rows, cols), jnp.float32),
        )
        averaged = total / jnp.full((rows, cols), end - begin, jnp.int32).astype(jnp.float32)
        new = outer_decay * mom[module] + averaged
        state[module] = new
        pltpu.make_async_copy(state.at[module], new_state.at[module, half], sems.at[4]).start()
        weights = mas[module].astype(jnp.float32)
        updated[module] = (weights - outer_rate * (averaged + outer_decay * new)).astype(
            jnp.bfloat16
        )

        @pl.loop(begin, end)
        def _(i):
            pltpu.make_async_copy(
                updated.at[module], sending.at[order[i], half], sems.at[3]
            ).start()

    wait_bytes(got, sems.at[3])
    wait_bytes(state, sems.at[4])


def outer(half, module_of, order, received, master, momentum, earlier):
    paths, rows, cols = received.shape
    modules = master.shape[0]
    f32, bf16 = jnp.float32, jnp.bfloat16
    operands = (module_of, order, received, master, momentum) + earlier
    return pl.pallas_call(
        functools.partial(outer_kernel, half),
        out_shape=(
            jax.ShapeDtypeStruct(momentum.shape, f32),
            jax.ShapeDtypeStruct((paths, 2, rows, cols), bf16),
        ),
        in_specs=[SMEM, SMEM] + [ANY] * (len(operands) - 2),
        out_specs=(ANY, ANY),
        scratch_shapes=[
            pltpu.VMEM((paths, rows, cols), bf16),
            pltpu.VMEM((modules, rows, cols), bf16),
            pltpu.VMEM((modules, rows, cols), f32),
            pltpu.VMEM((modules, rows, cols), f32),
            pltpu.VMEM((modules, rows, cols), bf16),
            pltpu.SMEM((modules + 1,), jnp.int32),
            pltpu.SemaphoreType.DMA((5,)),
        ],
        input_output_aliases={5: 0, 6: 1} if earlier else {},
        compiler_params=params(),
        cost_estimate=cost(paths * rows * cols, 4 * paths * rows * cols),
        name="outer",
    )(*operands)


def home_kernel(groups, owner, back, out, buf, sems):
    halves, blocks = out.shape[:2]
    per = blocks // groups
    parts = [(half, pl.ds(g * per, per)) for half in range(halves) for g in range(groups)]
    for i, (half, part) in enumerate(parts):

        @pl.loop(0, per)
        def _(step):
            block = part.start + step
            pltpu.make_async_copy(
                back.at[owner[block], half], buf.at[half, block], sems.at[i]
            ).start()

    stores = []
    for i, (half, part) in enumerate(parts):
        wait_bytes(buf.at[half, part], sems.at[i])
        store = pltpu.make_async_copy(
            buf.at[half, part], out.at[half, part], sems.at[len(parts) + i]
        )
        store.start()
        stores.append(store)
    for store in stores:
        store.wait()


def bring_home(owner, back):
    paths, halves, rows, cols = back.shape
    shape = (halves, paths, rows, cols)
    groups = 4
    return pl.pallas_call(
        functools.partial(home_kernel, groups),
        out_shape=jax.ShapeDtypeStruct(shape, back.dtype),
        in_specs=[SMEM, ANY],
        out_specs=ANY,
        scratch_shapes=[
            pltpu.VMEM(shape, back.dtype),
            pltpu.SemaphoreType.DMA((2 * halves * groups,)),
        ],
        compiler_params=params(),
        cost_estimate=cost(0, 4 * paths * halves * rows * cols),
        name="bring_home",
    )(owner, back)


def collect(tokens, grads):
    count = lax.axis_size("fsdp")
    right = [(i, (i + 1) % count) for i in range(count)]
    left = [(i, (i - 1) % count) for i in range(count)]
    tok_left = lax.ppermute(tokens, "fsdp", right)
    grd_right = lax.ppermute(grads, "fsdp", left)
    grd_left = lax.ppermute(grads, "fsdp", right)
    tok_right = lax.ppermute(tokens, "fsdp", left)
    grd_far = lax.ppermute(grd_right, "fsdp", left)
    tok_far = lax.ppermute(tok_left, "fsdp", right)
    return (
        jnp.concatenate([tokens, tok_left, tok_right, tok_far]),
        jnp.concatenate([grads, grd_left, grd_right, grd_far]),
    )


def exchange(blocks):
    return lax.all_to_all(blocks, "path", split_axis=0, concat_axis=0, tiled=True)


def shards(inputs, cotangent, master, momentum, sharing, block_owner):
    block_cols = master.shape[3]
    module_of = sharing[:, 0]
    order = jnp.argsort(module_of)
    tokens_all, grads_all = collect(inputs, cotangent)
    tok_rows, model_width = tokens_all.shape
    hidden_units = block_cols * lax.axis_size("fsdp")
    scales = (
        1.0 / math.sqrt(model_width),
        1.0 / math.sqrt(hidden_units),
        inner_rate / math.sqrt(tok_rows),
    )
    arrived = exchange(pick(module_of, master))
    down = delta_down(scales, block_owner, arrived, tokens_all, grads_all.T)
    got_down = exchange(down)
    up = delta_up(scales, block_owner, arrived, tokens_all, grads_all, tokens_all.T, down)
    got_up = exchange(up)
    earlier = outer(1, module_of, order, got_down, master, momentum, ())
    new_state, sending = outer(0, module_of, order, got_up, master, momentum, tuple(earlier))
    own_module = bring_home(block_owner, exchange(sending))
    return (new_state, own_module.reshape(1, 2, model_width, block_cols))


def solution(mesh):
    placed = (
        P(("path", "fsdp"), None),
        P(("path", "fsdp"), None),
        P(None, None, "path", "fsdp"),
        P(None, None, "path", "fsdp"),
        P(),
        P(),
    )
    return jax.shard_map(
        shards,
        mesh=mesh,
        in_specs=placed,
        out_specs=(P(None, None, "path", "fsdp"), P("path", None, None, "fsdp")),
        check_vma=False,
    )
```

```python
import functools
import math

import jax
import jax.numpy as jnp
from jax import lax
from jax.experimental import pallas as pl
from jax.experimental.pallas import tpu as pltpu
from jax.sharding import PartitionSpec as P

inner_rate = 10.0
outer_rate = 0.7
outer_decay = 0.9

VMEM_LIMIT = 56 * 1024 * 1024
FIRST_LIMIT = 24 * 1024 * 1024
ANY = pl.BlockSpec(memory_space=pl.ANY)
SMEM = pl.BlockSpec(memory_space=pltpu.SMEM)
VMEM = pl.BlockSpec(memory_space=pltpu.VMEM)


def params(limit=VMEM_LIMIT):
    return pltpu.CompilerParams(vmem_limit_bytes=limit)


def cost(flops, moved):
    return pl.CostEstimate(flops=flops, bytes_accessed=moved, transcendentals=0)


def wait_bytes(ref, sem):
    pltpu.make_async_copy(ref, ref, sem).wait()


def f32_dot(left, right):
    return jnp.dot(left, right, preferred_element_type=jnp.float32)


def pick_kernel(module_of, stored, out, sem):
    @pl.loop(0, out.shape[0], unroll=8)
    def _(path):
        pltpu.make_async_copy(stored.at[module_of[path]], out.at[path], sem).start()

    wait_bytes(out, sem)


def pick(module_of, stored):
    paths = module_of.shape[0]
    shape = (paths,) + stored.shape[1:]
    return pl.pallas_call(
        pick_kernel,
        out_shape=jax.ShapeDtypeStruct(shape, stored.dtype),
        in_specs=[SMEM, VMEM],
        out_specs=ANY,
        scratch_shapes=[pltpu.SemaphoreType.DMA],
        compiler_params=params(),
        cost_estimate=cost(0, 2 * math.prod(shape)),
        name="pick",
    )(module_of, stored)


def slabs_of(cols, cut):
    first = [(1, 0)]
    rest = [(1, c) for c in range(cut, cols, cut)] + [(0, c) for c in range(0, cols, cut)]
    return first, rest


def load_logical(owner, arrived, half, cols, weight, sem):
    rows = arrived.shape[2]

    @pl.loop(0, arrived.shape[0], unroll=8)
    def _(block):
        pltpu.make_async_copy(
            arrived.at[owner[block], half, :, cols],
            weight.at[pl.ds(pl.multiple_of(block * rows, rows), rows)],
            sem,
        ).start()


def sigmoid(values):
    return 1.0 / (1.0 + jnp.exp(-values))


def delta_rows(owner, left, pieces, rate, delta, out, sem, tile):
    rows = out.shape[2]

    @pl.loop(0, delta.shape[1] // tile)
    def _(step):
        at = pl.ds(pl.multiple_of(step * tile, tile), tile)
        for slab, (lhs, rhs, cols, scale) in enumerate(pieces):
            grad = f32_dot(lhs[at, :], rhs[:, cols]) * scale
            delta[slab, at, :] = (grad * rate).astype(jnp.bfloat16)

        @pl.loop(0, tile // rows, unroll=8)
        def _(inner):
            block = step * (tile // rows) + inner
            pltpu.make_async_copy(
                delta.at[:, pl.ds(pl.multiple_of(block * rows, rows), rows)],
                out.at[owner[block]],
                sem,
            ).start()

    wait_bytes(delta, sem)


def first_kernel(scales, owner, arrived, tokens, grads_t, out, weight, act, delta, sems):
    scale_in, scale_hid, rate = scales
    cut = act.shape[1]
    load_logical(owner, arrived, 0, pl.ds(0, cut), weight, sems.at[0])
    wait_bytes(weight, sems.at[0])
    part = act.shape[0] // 2

    @pl.loop(0, 2)
    def _(step):
        at = pl.ds(pl.multiple_of(step * part, part), part)
        pre = f32_dot(tokens[at, :], weight[...]) * scale_in
        act[at, :] = (pre * sigmoid(pre)).astype(jnp.bfloat16)

    pieces = [(grads_t, act, pl.ds(0, cut), scale_hid)]
    delta_rows(owner, grads_t, pieces, rate, delta, out, sems.at[1], 512)


def rest_kernel(
    scales, slabs, owner, arrived, tokens, grads, tokens_t, grads_t, earlier, out,
    up_weight, down_weight, tok, grd, tok_t, grd_t, act, slope, delta, sems,
):
    scale_in, scale_hid, rate = scales
    cols = slope.shape[1]
    cut = delta.shape[2]
    skip = cols - act.shape[1]
    pairs = [(tokens, tok), (grads, grd), (tokens_t, tok_t), (grads_t, grd_t)]
    copies = [
        pltpu.make_async_copy(source, target, sems.at[3 + i])
        for i, (source, target) in enumerate(pairs)
    ]
    for copy in copies:
        copy.start()
    load_logical(owner, arrived, 0, pl.ds(0, cols), up_weight, sems.at[0])
    load_logical(owner, arrived, 1, pl.ds(0, cols), down_weight, sems.at[1])
    wait_bytes(up_weight, sems.at[0])
    wait_bytes(down_weight, sems.at[1])
    for copy in copies:
        copy.wait()
    part = slope.shape[0] // 2
    for c in range(0, cols, cut):

        @pl.loop(0, 2)
        def _(step):
            at = pl.ds(pl.multiple_of(step * part, part), part)
            pre = f32_dot(tok[at, :], up_weight[:, pl.ds(c, cut)]) * scale_in
            back = f32_dot(grd[at, :], down_weight[:, pl.ds(c, cut)]) * scale_hid
            sig = sigmoid(pre)
            if c >= skip:
                act[at, pl.ds(c - skip, cut)] = (pre * sig).astype(jnp.bfloat16)
            slope[at, pl.ds(c, cut)] = (back * (sig * (1.0 + pre * (1.0 - sig)))).astype(
                jnp.bfloat16
            )

    pieces = [
        (tok_t, slope, pl.ds(c, cut), scale_in)
        if half == 0
        else (grd_t, act, pl.ds(c - skip, cut), scale_hid)
        for half, c in slabs
    ]
    delta_rows(owner, tok_t, pieces, rate, delta, out, sems.at[2], 512)


def delta_first(scales, cut, owner, arrived, tokens, grads_t):
    paths, _, rows, _ = arrived.shape
    count, width = tokens.shape
    bf16 = jnp.bfloat16
    return pl.pallas_call(
        functools.partial(first_kernel, scales),
        out_shape=jax.ShapeDtypeStruct((paths, 1, rows, cut), bf16),
        in_specs=[SMEM, ANY, VMEM, VMEM],
        out_specs=ANY,
        scratch_shapes=[
            pltpu.VMEM((width, cut), bf16),
            pltpu.VMEM((count, cut), bf16),
            pltpu.VMEM((1, width, cut), bf16),
            pltpu.SemaphoreType.DMA((2,)),
        ],
        compiler_params=params(FIRST_LIMIT),
        cost_estimate=cost(4 * count * width * cut, 4 * (2 * count * width + 2 * width * cut)),
        name="delta_first",
    )(owner, arrived, tokens, grads_t)


def delta_rest(scales, cut, slabs, owner, arrived, tokens, grads, tokens_t, grads_t, earlier):
    paths, _, rows, cols = arrived.shape
    count, width = tokens.shape
    bf16 = jnp.bfloat16
    return pl.pallas_call(
        functools.partial(rest_kernel, scales, slabs),
        out_shape=jax.ShapeDtypeStruct((paths, len(slabs), rows, cut), bf16),
        in_specs=[SMEM] + [ANY] * 6,
        out_specs=ANY,
        scratch_shapes=[
            pltpu.VMEM((width, cols), bf16),
            pltpu.VMEM((width, cols), bf16),
            pltpu.VMEM((count, width), bf16),
            pltpu.VMEM((count, width), bf16),
            pltpu.VMEM((width, count), bf16),
            pltpu.VMEM((width, count), bf16),
            pltpu.VMEM((count, cols - cut), bf16),
            pltpu.VMEM((count, cols), bf16),
            pltpu.VMEM((len(slabs), width, cut), bf16),
            pltpu.SemaphoreType.DMA((7,)),
        ],
        compiler_params=params(),
        cost_estimate=cost(8 * count * width * cols, 4 * (4 * count * width + 3 * width * cols)),
        name="delta_rest",
    )(owner, arrived, tokens, grads, tokens_t, grads_t, earlier)


def begin_of(module_of, first):
    modules = first.shape[0] - 1
    for module in range(modules + 1):
        first[module] = 0

    @pl.loop(0, module_of.shape[0])
    def _(path):
        first[module_of[path] + 1] += 1

    for module in range(modules):
        first[module + 1] += first[module]


def step_module(module, begin, end, order, got, slabs, mas, mom, state, updated):
    _, _, rows, cut = got.shape
    totals = lax.fori_loop(
        begin,
        end,
        lambda i, acc: tuple(
            a + got[order[i], s].astype(jnp.float32) for s, a in enumerate(acc)
        ),
        tuple(jnp.zeros((rows, cut), jnp.float32) for _ in slabs),
    )
    count = jnp.full((rows, cut), end - begin, jnp.int32).astype(jnp.float32)
    for (half, c), total in zip(slabs, totals, strict=True):
        at = (module, half, slice(None), pl.ds(c, cut))
        averaged = total / count
        new = outer_decay * mom[at] + averaged
        state[at] = new
        weights = mas[at].astype(jnp.float32)
        updated[at] = (weights - outer_rate * (averaged + outer_decay * new)).astype(
            jnp.bfloat16
        )


def outer_first_kernel(
    slabs, module_of, order, received, master, momentum, state_out, updated_out,
    got, mas, mom, state, updated, first, sems,
):
    ((half, c),) = slabs
    cut = got.shape[3]
    copies = [
        pltpu.make_async_copy(received, got, sems.at[0]),
        pltpu.make_async_copy(master.at[:, pl.ds(half, 1), :, pl.ds(c, cut)], mas, sems.at[1]),
        pltpu.make_async_copy(
            momentum.at[:, pl.ds(half, 1), :, pl.ds(c, cut)], mom, sems.at[2]
        ),
    ]
    for copy in copies:
        copy.start()
    begin_of(module_of, first)
    for copy in copies:
        copy.wait()

    @pl.loop(0, state.shape[0])
    def _(module):
        step_module(
            module, first[module], first[module + 1], order, got, [(0, 0)], mas, mom, state, updated
        )

    stores = [
        pltpu.make_async_copy(state, state_out, sems.at[0]),
        pltpu.make_async_copy(updated, updated_out, sems.at[1]),
    ]
    for store in stores:
        store.start()
    for store in stores:
        store.wait()


def outer_first(slabs, module_of, order, received, master, momentum):
    paths, _, rows, cut = received.shape
    modules = master.shape[0]
    f32, bf16 = jnp.float32, jnp.bfloat16
    shape = (modules, 1, rows, cut)
    return pl.pallas_call(
        functools.partial(outer_first_kernel, slabs),
        out_shape=(jax.ShapeDtypeStruct(shape, f32), jax.ShapeDtypeStruct(shape, bf16)),
        in_specs=[SMEM, SMEM, ANY, ANY, ANY],
        out_specs=(ANY, ANY),
        scratch_shapes=[
            pltpu.VMEM(received.shape, bf16),
            pltpu.VMEM(shape, bf16),
            pltpu.VMEM(shape, f32),
            pltpu.VMEM(shape, f32),
            pltpu.VMEM(shape, bf16),
            pltpu.SMEM((modules + 1,), jnp.int32),
            pltpu.SemaphoreType.DMA((3,)),
        ],
        compiler_params=params(),
        cost_estimate=cost(paths * rows * cut, 4 * paths * rows * cut),
        name="outer_first",
    )(module_of, order, received, master, momentum)


def outer_rest_kernel(
    slabs, module_of, order, received, master, momentum, state_first, updated_first,
    new_state, sending, got, mas, mom, state, updated, first, sems,
):
    modules = state.shape[0]
    cut = got.shape[3]
    early = (slice(None), pl.ds(1, 1), slice(None), pl.ds(0, cut))
    copies = [
        pltpu.make_async_copy(received, got, sems.at[0]),
        pltpu.make_async_copy(master, mas, sems.at[1]),
        pltpu.make_async_copy(momentum, mom, sems.at[2]),
        pltpu.make_async_copy(state_first, state.at[early], sems.at[3]),
        pltpu.make_async_copy(updated_first, updated.at[early], sems.at[4]),
    ]
    for copy in copies:
        copy.start()
    begin_of(module_of, first)
    for copy in copies:
        copy.wait()

    @pl.loop(0, modules)
    def _(module):
        begin, end = first[module], first[module + 1]
        step_module(module, begin, end, order, got, slabs, mas, mom, state, updated)
        pltpu.make_async_copy(state.at[module], new_state.at[module], sems.at[5]).start()

        @pl.loop(begin, end)
        def _(i):
            pltpu.make_async_copy(updated.at[module], sending.at[order[i]], sems.at[6]).start()

    wait_bytes(sending, sems.at[6])
    wait_bytes(state, sems.at[5])


def outer_rest(slabs, module_of, order, received, master, momentum, earlier):
    paths, _, rows, _ = received.shape
    modules, halves, _, cols = master.shape
    f32, bf16 = jnp.float32, jnp.bfloat16
    return pl.pallas_call(
        functools.partial(outer_rest_kernel, slabs),
        out_shape=(
            jax.ShapeDtypeStruct(momentum.shape, f32),
            jax.ShapeDtypeStruct((paths, halves, rows, cols), bf16),
        ),
        in_specs=[SMEM, SMEM] + [ANY] * 5,
        out_specs=(ANY, ANY),
        scratch_shapes=[
            pltpu.VMEM(received.shape, bf16),
            pltpu.VMEM(master.shape, bf16),
            pltpu.VMEM(momentum.shape, f32),
            pltpu.VMEM(momentum.shape, f32),
            pltpu.VMEM(master.shape, bf16),
            pltpu.SMEM((modules + 1,), jnp.int32),
            pltpu.SemaphoreType.DMA((7,)),
        ],
        compiler_params=params(),
        cost_estimate=cost(paths * rows * cols, 4 * paths * rows * cols),
        name="outer_rest",
    )(module_of, order, received, master, momentum, *earlier)


def home_kernel(groups, owner, back, out, buf, sems):
    per = out.shape[1] // groups
    for group in range(groups):

        @pl.loop(group * per, (group + 1) * per, unroll=8)
        def _(block):
            pltpu.make_async_copy(
                back.at[owner[block]], buf.at[:, block], sems.at[group]
            ).start()

    stores = []
    for group in range(groups):
        part = pl.ds(group * per, per)
        wait_bytes(buf.at[:, part], sems.at[group])
        store = pltpu.make_async_copy(
            buf.at[:, part], out.at[:, part], sems.at[groups + group]
        )
        store.start()
        stores.append(store)
    for store in stores:
        store.wait()


def bring_home(owner, back):
    paths, halves, rows, cols = back.shape
    shape = (halves, paths, rows, cols)
    groups = 4
    return pl.pallas_call(
        functools.partial(home_kernel, groups),
        out_shape=jax.ShapeDtypeStruct(shape, back.dtype),
        in_specs=[SMEM, ANY],
        out_specs=ANY,
        scratch_shapes=[
            pltpu.VMEM(shape, back.dtype),
            pltpu.SemaphoreType.DMA((2 * groups,)),
        ],
        compiler_params=params(),
        cost_estimate=cost(0, 4 * paths * halves * rows * cols),
        name="bring_home",
    )(owner, back)


def collect(tokens, grads):
    count = lax.axis_size("fsdp")
    right = [(i, (i + 1) % count) for i in range(count)]
    left = [(i, (i - 1) % count) for i in range(count)]
    tok_left = lax.ppermute(tokens, "fsdp", right)
    grd_right = lax.ppermute(grads, "fsdp", left)
    grd_left = lax.ppermute(grads, "fsdp", right)
    tok_right = lax.ppermute(tokens, "fsdp", left)
    grd_far = lax.ppermute(grd_right, "fsdp", left)
    tok_far = lax.ppermute(tok_left, "fsdp", right)
    return (
        jnp.concatenate([tokens, tok_left, tok_right, tok_far]),
        jnp.concatenate([grads, grd_left, grd_right, grd_far]),
    )


def exchange(blocks):
    return lax.all_to_all(blocks, "path", split_axis=0, concat_axis=0, tiled=True)


def shards(inputs, cotangent, master, momentum, sharing, block_owner):
    block_cols = master.shape[3]
    module_of = sharing[:, 0]
    order = jnp.argsort(module_of)
    tokens_all, grads_all = collect(inputs, cotangent)
    tok_rows, model_width = tokens_all.shape
    hidden_units = block_cols * lax.axis_size("fsdp")
    scales = (
        1.0 / math.sqrt(model_width),
        1.0 / math.sqrt(hidden_units),
        inner_rate / math.sqrt(tok_rows),
    )
    arrived = exchange(pick(module_of, master))
    cut = block_cols // 2
    early, late = slabs_of(block_cols, cut)
    grads_t = grads_all.T
    begun = delta_first(scales, cut, block_owner, arrived, tokens_all, grads_t)
    got_first = exchange(begun)
    rest = delta_rest(
        scales, cut, late, block_owner, arrived, tokens_all, grads_all, tokens_all.T, grads_t, begun
    )
    got_rest = exchange(rest)
    earlier = outer_first(early, module_of, order, got_first, master, momentum)
    new_state, sending = outer_rest(late, module_of, order, got_rest, master, momentum, earlier)
    own_module = bring_home(block_owner, exchange(sending))
    return (new_state, own_module.reshape(1, 2, model_width, block_cols))


def solution(mesh):
    placed = (
        P(("path", "fsdp"), None),
        P(("path", "fsdp"), None),
        P(None, None, "path", "fsdp"),
        P(None, None, "path", "fsdp"),
        P(),
        P(),
    )
    return jax.shard_map(
        shards,
        mesh=mesh,
        in_specs=placed,
        out_specs=(P(None, None, "path", "fsdp"), P("path", None, None, "fsdp")),
        check_vma=False,
    )
```

```python
import functools
import math

import jax
import jax.numpy as jnp
from jax import lax
from jax.experimental import pallas as pl
from jax.experimental.pallas import tpu as pltpu
from jax.sharding import PartitionSpec as P

inner_rate = 10.0
outer_rate = 0.7
outer_decay = 0.9

VMEM_LIMIT = 56 * 1024 * 1024
MAIN_LIMIT = 40 * 1024 * 1024
OUTER_LIMIT = 40 * 1024 * 1024
LAST_LIMIT = 36 * 1024 * 1024
ANY = pl.BlockSpec(memory_space=pl.ANY)
SMEM = pl.BlockSpec(memory_space=pltpu.SMEM)
VMEM = pl.BlockSpec(memory_space=pltpu.VMEM)


def params(limit=VMEM_LIMIT):
    return pltpu.CompilerParams(vmem_limit_bytes=limit)


def cost(flops, moved):
    return pl.CostEstimate(flops=flops, bytes_accessed=moved, transcendentals=0)


def wait_bytes(ref, sem):
    pltpu.make_async_copy(ref, ref, sem).wait()


def f32_dot(left, right):
    return jnp.dot(left, right, preferred_element_type=jnp.float32)


def pick_kernel(pieces, module_of, stored, out, held, sem, load_sems):
    at, loads = 0, []
    for i, (half, col, cols) in enumerate(pieces):
        loads.append(
            pltpu.make_async_copy(
                stored.at[:, half, :, pl.ds(col, cols)],
                held.at[:, :, pl.ds(at, cols)],
                load_sems.at[i],
            )
        )
        loads[-1].start()
        at += cols
    for load in loads:
        load.wait()

    @pl.loop(0, out.shape[0], unroll=8)
    def _(path):
        pltpu.make_async_copy(held.at[module_of[path]], out.at[path], sem).start()

    wait_bytes(out, sem)


def pick(pieces, module_of, stored):
    paths, (modules, _, rows, _) = module_of.shape[0], stored.shape
    cols = sum(piece[2] for piece in pieces)
    return pl.pallas_call(
        functools.partial(pick_kernel, pieces),
        out_shape=jax.ShapeDtypeStruct((paths, rows, cols), stored.dtype),
        in_specs=[SMEM, ANY],
        out_specs=ANY,
        scratch_shapes=[
            pltpu.VMEM((modules, rows, cols), stored.dtype),
            pltpu.SemaphoreType.DMA,
            pltpu.SemaphoreType.DMA((len(pieces),)),
        ],
        compiler_params=params(),
        cost_estimate=cost(0, 2 * paths * rows * cols),
        name="pick",
    )(module_of, stored)


def sigmoid(values):
    return 1.0 / (1.0 + jnp.exp(-values))


def starter(sems):
    def start(source, target, sem):
        copy = pltpu.make_async_copy(source, target, sems.at[sem])
        copy.start()
        return copy

    return start


def load_shards(start, shards_in, target, first_sem):
    each = shards_in[0].shape[0]
    return [
        start(shard, target.at[pl.ds(i * each, each)], first_sem + i)
        for i, shard in enumerate(shards_in)
    ]


def main_kernel(
    scales, late, owner, arrived, tokens_t, grads_t, *refs,
):
    scale_in, scale_hid, rate = scales
    count = 4
    tok_in, grd_in = refs[:count], refs[count : 2 * count]
    (
        out, grd, tok_t, factor,
        weight, tok, grd_t, act, slope, up, down, sems,
    ) = refs[2 * count :]
    rows, cols = out.shape[2:]
    early = cols - late
    start = starter(sems)
    toks = load_shards(start, tok_in[:2], tok, 4)

    @pl.loop(0, arrived.shape[0], unroll=8)
    def _(block):
        pltpu.make_async_copy(
            arrived.at[owner[block]],
            weight.at[pl.ds(pl.multiple_of(block * rows, rows), rows)],
            sems.at[0],
        ).start()

    grds = load_shards(start, grd_in[:2], grd, 4 + count)
    half = tok.shape[0] // 2
    toks += load_shards(start, tok_in[2:], tok.at[pl.ds(half, half)], 6)
    grds += load_shards(start, grd_in[2:], grd.at[pl.ds(half, half)], 6 + count)
    grd_t_copy = start(grads_t, grd_t, 2)
    tok_t_copy = start(tokens_t, tok_t, 3)
    wait_bytes(weight, sems.at[0])
    mid = cols // 2
    for part in range(2):
        at = pl.ds(part * half, half)
        for copy in toks[2 * part : 2 * part + 2] + grds[2 * part : 2 * part + 2]:
            copy.wait()
        for col, width, known in ((0, mid, mid), (mid, cols - mid, early - mid)):
            pre = f32_dot(tok[at, :], weight[:, pl.ds(col, width)]) * scale_in
            back = f32_dot(grd[at, :], weight[:, pl.ds(cols + col, known)]) * scale_hid
            sig = sigmoid(pre)
            act[at, pl.ds(col, width)] = (pre * sig).astype(jnp.bfloat16)
            turn = sig * (1.0 + pre * (1.0 - sig))
            slope[at, pl.ds(col, known)] = (back * turn[:, :known]).astype(jnp.bfloat16)
            if known < width:
                factor[at, :] = turn[:, known:]
    grd_t_copy.wait()
    tok_t_copy.wait()
    tile = 512

    @pl.loop(0, down.shape[0] // tile)
    def _(step):
        at = pl.ds(pl.multiple_of(step * tile, tile), tile)
        down[at, :] = (f32_dot(grd_t[at, :], act[...]) * scale_hid * rate).astype(jnp.bfloat16)
        up[at, :] = (f32_dot(tok_t[at, :], slope[...]) * scale_in * rate).astype(jnp.bfloat16)

        @pl.loop(0, tile // rows, unroll=8)
        def _(inner):
            block = step * (tile // rows) + inner
            at = pl.ds(pl.multiple_of(block * rows, rows), rows)
            place = owner[block]
            pltpu.make_async_copy(down.at[at], out.at[place, 1], sems.at[2]).start()
            pltpu.make_async_copy(
                up.at[at], out.at[place, 0, :, pl.ds(0, early)], sems.at[3]
            ).start()

    wait_bytes(down, sems.at[2])
    wait_bytes(up, sems.at[3])


def main_delta(scales, late, owner, arrived, tokens, grads, tokens_t, grads_t):
    paths, rows, both = arrived.shape
    width, count = tokens_t.shape
    cols = (both + late) // 2
    f32, bf16 = jnp.float32, jnp.bfloat16
    return pl.pallas_call(
        functools.partial(main_kernel, scales, late),
        out_shape=(
            pltpu.HBM((paths, 2, rows, cols), bf16),
            pltpu.VMEM((count, width), bf16),
            pltpu.VMEM((width, count), bf16),
            pltpu.VMEM((count, late), f32),
        ),
        in_specs=[SMEM] + [ANY] * 11,
        out_specs=(ANY, VMEM, VMEM, VMEM),
        scratch_shapes=[
            pltpu.VMEM((width, both), bf16),
            pltpu.VMEM((count, width), bf16),
            pltpu.VMEM((width, count), bf16),
            pltpu.VMEM((count, cols), bf16),
            pltpu.VMEM((count, cols - late), bf16),
            pltpu.VMEM((width, cols - late), bf16),
            pltpu.VMEM((width, cols), bf16),
            pltpu.SemaphoreType.DMA((12,)),
        ],
        compiler_params=params(MAIN_LIMIT),
        cost_estimate=cost(8 * count * width * cols, 8 * (count * width + width * cols)),
        name="main_delta",
    )(owner, arrived, tokens_t, grads_t, *tokens, *grads)


def last_kernel(
    scales, owner, arrived, grads, tokens_t, factor, begun, out, got, weight, sending, sems
):
    scale_in, scale_hid, rate = scales
    blocks, rows, late = got.shape
    start = starter(sems)
    start(arrived, got, 0).wait()

    @pl.loop(0, blocks, unroll=4)
    def _(block):
        weight[pl.ds(pl.multiple_of(block * rows, rows), rows), :] = got[owner[block]]

    back = f32_dot(grads[...], weight[...]) * scale_hid
    slope = (back * factor[...]).astype(jnp.bfloat16)
    weight[...] = (f32_dot(tokens_t[...], slope) * scale_in * rate).astype(jnp.bfloat16)

    @pl.loop(0, blocks, unroll=4)
    def _(block):
        sending[owner[block]] = weight[pl.ds(pl.multiple_of(block * rows, rows), rows), :]

    start(sending, out.at[:, 0, :, pl.ds(out.shape[3] - late, late)], 1).wait()


def last_delta(scales, owner, arrived, begun, grads, tokens_t, factor):
    paths, rows, late = arrived.shape
    width, count = tokens_t.shape
    bf16 = jnp.bfloat16
    return pl.pallas_call(
        functools.partial(last_kernel, scales),
        out_shape=pltpu.HBM(begun.shape, bf16),
        in_specs=[SMEM, ANY, VMEM, VMEM, VMEM, ANY],
        out_specs=ANY,
        scratch_shapes=[
            pltpu.VMEM((paths, rows, late), bf16),
            pltpu.VMEM((width, late), bf16),
            pltpu.VMEM((paths, rows, late), bf16),
            pltpu.SemaphoreType.DMA((2,)),
        ],
        input_output_aliases={5: 0},
        compiler_params=params(LAST_LIMIT),
        cost_estimate=cost(4 * count * width * late, 4 * count * width),
        name="last_delta",
    )(owner, arrived, grads, tokens_t, factor, begun)


def ready_kernel(module_of, master, momentum, base, kept, share, first, mas, mom, sems):
    copies = [
        pltpu.make_async_copy(master, mas, sems.at[0]),
        pltpu.make_async_copy(momentum, mom, sems.at[1]),
    ]
    for copy in copies:
        copy.start()
    modules = first.shape[0] - 1
    for module in range(modules + 1):
        first[module] = 0

    @pl.loop(0, module_of.shape[0])
    def _(path):
        first[module_of[path] + 1] += 1

    for module in range(modules):
        count = jnp.full(share.shape[1:], first[module + 1], jnp.int32)
        share[module] = 1.0 / count.astype(jnp.float32)
        first[module + 1] += first[module]
    for copy in copies:
        copy.wait()

    @pl.loop(0, modules)
    def _(module):
        old = outer_decay * mom[module]
        kept[module] = old
        base[module] = mas[module].astype(jnp.float32) - (outer_rate * outer_decay) * old


def ready(module_of, master, momentum):
    f32 = jnp.float32
    modules = master.shape[0]
    return pl.pallas_call(
        ready_kernel,
        out_shape=(
            pltpu.VMEM(momentum.shape, f32),
            pltpu.VMEM(momentum.shape, f32),
            pltpu.VMEM((modules, 8, momentum.shape[3]), f32),
            jax.ShapeDtypeStruct((modules + 1,), jnp.int32),
        ),
        in_specs=[SMEM, ANY, ANY],
        out_specs=(VMEM, VMEM, VMEM, SMEM),
        scratch_shapes=[
            pltpu.VMEM(master.shape, master.dtype),
            pltpu.VMEM(momentum.shape, f32),
            pltpu.SemaphoreType.DMA((2,)),
        ],
        compiler_params=params(OUTER_LIMIT),
        cost_estimate=cost(0, 8 * momentum.size),
        name="ready",
    )(module_of, master, momentum)


def outer_kernel(
    first, order, received, base, kept, share, new_state, sending, got, state, updated, sems
):
    modules, halves, rows, cols = state.shape
    step = outer_rate * (1.0 + outer_decay)
    loads = [
        pltpu.make_async_copy(received.at[:, half], got.at[half], sems.at[half])
        for half in range(halves)
    ]
    for load in loads:
        load.start()
    for half in range(halves):
        loads[half].wait()

        @pl.loop(0, modules)
        def _(module):
            begin, end = first[module], first[module + 1]
            total = lax.fori_loop(
                begin,
                end,
                lambda i, acc: acc + got[half, order[i]].astype(jnp.float32),
                jnp.zeros((rows, cols), jnp.float32),
            )
            averaged = (total.reshape(-1, 8, cols) * share[module]).reshape(rows, cols)
            state[module, half] = kept[module, half] + averaged
            updated[module, half] = (base[module, half] - step * averaged).astype(jnp.bfloat16)
            if half == halves - 1:
                pltpu.make_async_copy(
                    state.at[module], new_state.at[module], sems.at[halves]
                ).start()

                @pl.loop(begin, end)
                def _(i):
                    pltpu.make_async_copy(
                        updated.at[module], sending.at[order[i]], sems.at[halves + 1]
                    ).start()

    wait_bytes(sending, sems.at[halves + 1])
    wait_bytes(state, sems.at[halves])


def outer(first, order, received, base, kept, share):
    paths, halves, rows, cols = received.shape
    f32, bf16 = jnp.float32, jnp.bfloat16
    return pl.pallas_call(
        outer_kernel,
        out_shape=(
            jax.ShapeDtypeStruct(kept.shape, f32),
            jax.ShapeDtypeStruct(received.shape, bf16),
        ),
        in_specs=[SMEM, SMEM, ANY, VMEM, VMEM, VMEM],
        out_specs=(ANY, ANY),
        scratch_shapes=[
            pltpu.VMEM((halves, paths, rows, cols), bf16),
            pltpu.VMEM(kept.shape, f32),
            pltpu.VMEM(kept.shape, bf16),
            pltpu.SemaphoreType.DMA((halves + 2,)),
        ],
        compiler_params=params(OUTER_LIMIT),
        cost_estimate=cost(2 * paths * rows * cols, 8 * paths * rows * cols),
        name="outer",
    )(first, order, received, base, kept, share)


def home_kernel(groups, owner, back, out, buf, place, sems):
    per = back.shape[0] // groups
    loads = []
    for group in range(groups):
        part = pl.ds(group * per, per)
        loads.append(
            pltpu.make_async_copy(back.at[part], buf.at[part], sems.at[group])
        )
        loads[-1].start()

    @pl.loop(0, back.shape[0], unroll=8)
    def _(block):
        place[owner[block]] = block

    for group in range(groups):
        loads[group].wait()

        @pl.loop(0, per, unroll=8)
        def _(inner):
            holder = group * per + inner
            pltpu.make_async_copy(
                buf.at[holder], out.at[:, place[holder]], sems.at[groups]
            ).start()

    wait_bytes(buf, sems.at[groups])


def bring_home(owner, back):
    paths, halves, rows, cols = back.shape
    groups = 4
    return pl.pallas_call(
        functools.partial(home_kernel, groups),
        out_shape=jax.ShapeDtypeStruct((halves, paths, rows, cols), back.dtype),
        in_specs=[SMEM, ANY],
        out_specs=ANY,
        scratch_shapes=[
            pltpu.VMEM(back.shape, back.dtype),
            pltpu.SMEM((paths,), jnp.int32),
            pltpu.SemaphoreType.DMA((groups + 1,)),
        ],
        compiler_params=params(),
        cost_estimate=cost(0, 4 * paths * halves * rows * cols),
        name="bring_home",
    )(owner, back)


def collect(tokens, grads):
    count = lax.axis_size("fsdp")
    right = [(i, (i + 1) % count) for i in range(count)]
    left = [(i, (i - 1) % count) for i in range(count)]
    tok_left = lax.ppermute(tokens, "fsdp", right)
    grd_right = lax.ppermute(grads, "fsdp", left)
    grd_left = lax.ppermute(grads, "fsdp", right)
    tok_right = lax.ppermute(tokens, "fsdp", left)
    grd_far = lax.ppermute(grd_right, "fsdp", left)
    tok_far = lax.ppermute(tok_left, "fsdp", right)
    return (tokens, tok_left, tok_right, tok_far), (grads, grd_left, grd_right, grd_far)


def exchange(blocks):
    return lax.all_to_all(blocks, "path", split_axis=0, concat_axis=0, tiled=True)


def shards(inputs, cotangent, master, momentum, sharing, block_owner):
    block_cols = master.shape[3]
    module_of = sharing[:, 0]
    order = jnp.argsort(module_of)
    fsdp = lax.axis_size("fsdp")
    rows, model_width = inputs.shape
    fill = ((0, -rows % 64), (0, 0))
    tokens, grads = collect(
        *lax.optimization_barrier((jnp.pad(inputs, fill), jnp.pad(cotangent, fill)))
    )
    tokens_t, grads_t = jnp.concatenate(tokens).T, jnp.concatenate(grads).T
    scales = (
        1.0 / math.sqrt(model_width),
        1.0 / math.sqrt(block_cols * fsdp),
        inner_rate / math.sqrt(rows * fsdp),
    )
    late = block_cols // 4
    early = block_cols - late
    arrived = exchange(pick([(0, 0, block_cols), (1, 0, early)], module_of, master))
    arrived_late = exchange(pick([(1, early, late)], module_of, master))
    held = main_delta(
        scales, late, block_owner, arrived, tokens, grads, tokens_t, grads_t
    )
    delta = last_delta(scales, block_owner, arrived_late, *held)
    base, kept, share, first = ready(module_of, master, momentum)
    new_state, sending = outer(first, order, exchange(delta), base, kept, share)
    own_module = bring_home(block_owner, exchange(sending))
    return (new_state, own_module.reshape(1, 2, model_width, block_cols))


def solution(mesh):
    placed = (
        P(("path", "fsdp"), None),
        P(("path", "fsdp"), None),
        P(None, None, "path", "fsdp"),
        P(None, None, "path", "fsdp"),
        P(),
        P(),
    )
    return jax.shard_map(
        shards,
        mesh=mesh,
        in_specs=placed,
        out_specs=(P(None, None, "path", "fsdp"), P("path", None, None, "fsdp")),
        check_vma=False,
    )
```

```python
import functools
import math

import jax
import jax.numpy as jnp
from jax import lax
from jax.experimental import pallas as pl
from jax.experimental.pallas import tpu as pltpu
from jax.sharding import PartitionSpec as P

inner_rate = 10.0
outer_rate = 0.7
outer_decay = 0.9

VMEM_LIMIT = 56 * 1024 * 1024
ANY = pl.BlockSpec(memory_space=pl.ANY)
SMEM = pl.BlockSpec(memory_space=pltpu.SMEM)
VMEM = pl.BlockSpec(memory_space=pltpu.VMEM)


def params():
    return pltpu.CompilerParams(vmem_limit_bytes=VMEM_LIMIT)


def cost(flops, moved):
    return pl.CostEstimate(flops=flops, bytes_accessed=moved, transcendentals=0)


def wait_bytes(ref, sem):
    pltpu.make_async_copy(ref, ref, sem).wait()


def f32_dot(left, right):
    return jnp.dot(left, right, preferred_element_type=jnp.float32)


def pick_kernel(module_of, stored, out, sem):
    @pl.loop(0, out.shape[0], unroll=8)
    def _(path):
        pltpu.make_async_copy(stored.at[module_of[path]], out.at[path], sem).start()

    wait_bytes(out, sem)


def pick(module_of, stored):
    paths = module_of.shape[0]
    shape = (paths,) + stored.shape[1:]
    return pl.pallas_call(
        pick_kernel,
        out_shape=jax.ShapeDtypeStruct(shape, stored.dtype),
        in_specs=[SMEM, VMEM],
        out_specs=ANY,
        scratch_shapes=[pltpu.SemaphoreType.DMA],
        compiler_params=params(),
        cost_estimate=cost(0, 2 * math.prod(shape)),
        name="pick",
    )(module_of, stored)


def sigmoid(values):
    return 1.0 / (1.0 + jnp.exp(-values))


def delta_kernel(scales, tiles, owner, arrived, order, tokens_t, grads_t, *refs):
    scale_in, scale_hid, rate = scales
    tile_cols, tile_rows = tiles
    tok_in, grd_in = refs[:4], refs[4:8]
    out, weight, tok, grd, tok_t, grd_t, act, slope, delta, sems = refs[8:]
    rows = arrived.shape[2]
    each = tok_in[0].shape[0]

    def start(source, target, sem):
        copy = pltpu.make_async_copy(source, target, sems.at[sem])
        copy.start()
        return copy

    def load(shards_in, target, i, sem):
        return start(shards_in[i], target.at[pl.ds(i * each, each)], sem + i)

    loads = [[load(tok_in, tok, 0, 4), load(tok_in, tok, 1, 4)]]

    @pl.loop(0, arrived.shape[0], unroll=8)
    def _(block):
        pltpu.make_async_copy(
            arrived.at[owner[block]],
            weight.at[:, pl.ds(pl.multiple_of(block * rows, rows), rows)],
            sems.at[0],
        ).start()

    loads[0] += [load(grd_in, grd, 0, 8), load(grd_in, grd, 1, 8)]
    wait_bytes(weight, sems.at[0])
    for part in range(2):
        at = pl.ds(part * 2 * each, 2 * each)
        for copy in loads[part]:
            copy.wait()
        if part == 0:
            loads.append([load(tok_in, tok, i, 4) for i in (2, 3)])
            loads[1] += [load(grd_in, grd, i, 8) for i in (2, 3)]
            late = [start(grads_t, grd_t, 2), start(tokens_t, tok_t, 3)]

        @pl.loop(0, act.shape[1] // tile_cols)
        def _(step):
            cols = pl.ds(pl.multiple_of(step * tile_cols, tile_cols), tile_cols)
            pre = f32_dot(tok[at, :], weight[0, :, cols]) * scale_in
            back = f32_dot(grd[at, :], weight[1, :, cols]) * scale_hid
            sig = sigmoid(pre)
            act[at, cols] = (pre * sig).astype(jnp.bfloat16)
            slope[at, cols] = (back * (sig * (1.0 + pre * (1.0 - sig)))).astype(jnp.bfloat16)

    for copy in late:
        copy.wait()

    @pl.loop(0, delta.shape[1] // tile_rows)
    def _(step):
        at = pl.ds(pl.multiple_of(step * tile_rows, tile_rows), tile_rows)
        grad_down = f32_dot(grd_t[at, :], act[...]) * scale_hid
        delta[1, at, :] = (grad_down * rate).astype(jnp.bfloat16)
        grad_up = f32_dot(tok_t[at, :], slope[...]) * scale_in
        delta[0, at, :] = (grad_up * rate).astype(jnp.bfloat16)

        @pl.loop(0, tile_rows // rows, unroll=8)
        def _(inner):
            block = step * (tile_rows // rows) + inner
            pltpu.make_async_copy(
                delta.at[:, pl.ds(pl.multiple_of(block * rows, rows), rows)],
                out.at[owner[block]],
                sems.at[1],
            ).start()

    wait_bytes(delta, sems.at[1])


def path_delta(scales, owner, arrived, order, tokens, grads, tokens_t, grads_t):
    _, halves, _, cols = arrived.shape
    width, count = tokens_t.shape
    bf16 = jnp.bfloat16
    return pl.pallas_call(
        functools.partial(delta_kernel, scales, (1024, 512)),
        out_shape=jax.ShapeDtypeStruct(arrived.shape, bf16),
        in_specs=[SMEM] + [ANY] * 12,
        out_specs=ANY,
        scratch_shapes=[
            pltpu.VMEM((halves, width, cols), bf16),
            pltpu.VMEM((count, width), bf16),
            pltpu.VMEM((count, width), bf16),
            pltpu.VMEM((width, count), bf16),
            pltpu.VMEM((width, count), bf16),
            pltpu.VMEM((count, cols), bf16),
            pltpu.VMEM((count, cols), bf16),
            pltpu.VMEM((halves, width, cols), bf16),
            pltpu.SemaphoreType.DMA((12,)),
        ],
        compiler_params=params(),
        cost_estimate=cost(8 * count * width * cols, 8 * (count * width + width * cols)),
        name="path_delta",
    )(owner, arrived, order, tokens_t, grads_t, *tokens, *grads)


def outer_kernel(
    module_of, order, received, master, momentum, new_state, sending,
    got, mas, mom, state, updated, share, first, sems,
):
    modules, halves, rows, cols = state.shape
    step = outer_rate * (1.0 + outer_decay)
    loads = []
    for half in range(halves):
        sources = (received.at[:, half], master.at[:, half], momentum.at[:, half])
        targets = (got.at[half], mas.at[half], mom.at[half])
        loads.append(
            [
                pltpu.make_async_copy(source, target, sems.at[3 * half + i])
                for i, (source, target) in enumerate(zip(sources, targets, strict=True))
            ]
        )
        for load in loads[half]:
            load.start()

    for module in range(modules + 1):
        first[module] = 0

    @pl.loop(0, module_of.shape[0], unroll=8)
    def _(path):
        first[module_of[path] + 1] += 1

    for module in range(modules):
        count = jnp.full(share.shape[1:], first[module + 1], jnp.int32)
        share[module] = 1.0 / count.astype(jnp.float32)
        first[module + 1] += first[module]

    for half in range(halves):
        for load in loads[half]:
            load.wait()

        @pl.loop(0, modules)
        def _(module):
            begin, end = first[module], first[module + 1]
            total = lax.fori_loop(
                begin,
                end,
                lambda i, acc: acc + got[half, order[i]].astype(jnp.float32),
                jnp.zeros((rows, cols), jnp.float32),
            )
            averaged = (total.reshape(-1, 8, cols) * share[module]).reshape(rows, cols)
            kept = outer_decay * mom[half, module]
            state[module, half] = kept + averaged
            weights = mas[half, module].astype(jnp.float32)
            updated[module, half] = (
                weights - (outer_rate * outer_decay) * kept - step * averaged
            ).astype(jnp.bfloat16)
            if half == halves - 1:
                pltpu.make_async_copy(
                    state.at[module], new_state.at[module], sems.at[6]
                ).start()

                @pl.loop(begin, end)
                def _(i):
                    pltpu.make_async_copy(
                        updated.at[module], sending.at[order[i]], sems.at[7]
                    ).start()

    wait_bytes(sending, sems.at[7])
    wait_bytes(state, sems.at[6])


def outer(module_of, order, received, master, momentum):
    paths, halves, rows, cols = received.shape
    modules = master.shape[0]
    f32, bf16 = jnp.float32, jnp.bfloat16
    return pl.pallas_call(
        outer_kernel,
        out_shape=(
            jax.ShapeDtypeStruct(momentum.shape, f32),
            jax.ShapeDtypeStruct(received.shape, bf16),
        ),
        in_specs=[SMEM, SMEM, ANY, ANY, ANY],
        out_specs=(ANY, ANY),
        scratch_shapes=[
            pltpu.VMEM((halves, paths, rows, cols), bf16),
            pltpu.VMEM((halves, modules, rows, cols), bf16),
            pltpu.VMEM((halves, modules, rows, cols), f32),
            pltpu.VMEM(momentum.shape, f32),
            pltpu.VMEM(master.shape, bf16),
            pltpu.VMEM((modules, 8, cols), f32),
            pltpu.SMEM((modules + 1,), jnp.int32),
            pltpu.SemaphoreType.DMA((8,)),
        ],
        compiler_params=params(),
        cost_estimate=cost(2 * paths * rows * cols, 8 * paths * rows * cols),
        name="outer",
    )(module_of, order, received, master, momentum)


def home_kernel(groups, owner, back, out, buf, place, sems):
    per = back.shape[0] // groups
    loads = []
    for group in range(groups):
        part = pl.ds(group * per, per)
        loads.append(
            pltpu.make_async_copy(back.at[part], buf.at[part], sems.at[group])
        )
        loads[-1].start()

    @pl.loop(0, back.shape[0], unroll=8)
    def _(block):
        place[owner[block]] = block

    for group in range(groups):
        loads[group].wait()

        @pl.loop(0, per, unroll=8)
        def _(inner):
            holder = group * per + inner
            pltpu.make_async_copy(
                buf.at[holder], out.at[:, place[holder]], sems.at[groups]
            ).start()

    wait_bytes(buf, sems.at[groups])


def bring_home(owner, back):
    paths, halves, rows, cols = back.shape
    groups = 4
    return pl.pallas_call(
        functools.partial(home_kernel, groups),
        out_shape=jax.ShapeDtypeStruct((halves, paths, rows, cols), back.dtype),
        in_specs=[SMEM, ANY],
        out_specs=ANY,
        scratch_shapes=[
            pltpu.VMEM(back.shape, back.dtype),
            pltpu.SMEM((paths,), jnp.int32),
            pltpu.SemaphoreType.DMA((groups + 1,)),
        ],
        compiler_params=params(),
        cost_estimate=cost(0, 4 * paths * halves * rows * cols),
        name="bring_home",
    )(owner, back)


def collect(tokens, grads):
    count = lax.axis_size("fsdp")
    right = [(i, (i + 1) % count) for i in range(count)]
    left = [(i, (i - 1) % count) for i in range(count)]
    tok_left = lax.ppermute(tokens, "fsdp", right)
    grd_right = lax.ppermute(grads, "fsdp", left)
    grd_left = lax.ppermute(grads, "fsdp", right)
    tok_right = lax.ppermute(tokens, "fsdp", left)
    grd_far = lax.ppermute(grd_right, "fsdp", left)
    tok_far = lax.ppermute(tok_left, "fsdp", right)
    return (tokens, tok_left, tok_right, tok_far), (grads, grd_left, grd_right, grd_far)


def exchange(blocks):
    return lax.all_to_all(blocks, "path", split_axis=0, concat_axis=0, tiled=True)


def shards(inputs, cotangent, master, momentum, sharing, block_owner):
    block_cols = master.shape[3]
    module_of = sharing[:, 0]
    order = jnp.argsort(module_of)
    fsdp = lax.axis_size("fsdp")
    rows, model_width = inputs.shape
    fill = ((0, -rows % 64), (0, 0))
    tokens, grads = collect(
        *lax.optimization_barrier((jnp.pad(inputs, fill), jnp.pad(cotangent, fill)))
    )
    tokens_t, grads_t = jnp.concatenate(tokens).T, jnp.concatenate(grads).T
    scales = (
        1.0 / math.sqrt(model_width),
        1.0 / math.sqrt(block_cols * fsdp),
        inner_rate / math.sqrt(rows * fsdp),
    )
    arrived = exchange(pick(module_of, master))
    delta = path_delta(
        scales, block_owner, arrived, order, tokens, grads, tokens_t, grads_t
    )
    new_state, sending = outer(module_of, order, exchange(delta), master, momentum)
    own_module = bring_home(block_owner, exchange(sending))
    return (new_state, own_module.reshape(1, 2, model_width, block_cols))


def solution(mesh):
    placed = (
        P(("path", "fsdp"), None),
        P(("path", "fsdp"), None),
        P(None, None, "path", "fsdp"),
        P(None, None, "path", "fsdp"),
        P(),
        P(),
    )
    return jax.shard_map(
        shards,
        mesh=mesh,
        in_specs=placed,
        out_specs=(P(None, None, "path", "fsdp"), P("path", None, None, "fsdp")),
        check_vma=False,
    )
```

```python
import functools
import math

import jax
import jax.numpy as jnp
from jax import lax
from jax.experimental import pallas as pl
from jax.experimental.pallas import tpu as pltpu
from jax.sharding import PartitionSpec as P

inner_rate = 10.0
outer_rate = 0.7
outer_decay = 0.9

VMEM_LIMIT = 56 * 1024 * 1024
ANY = pl.BlockSpec(memory_space=pl.ANY)
SMEM = pl.BlockSpec(memory_space=pltpu.SMEM)
VMEM = pl.BlockSpec(memory_space=pltpu.VMEM)


def params():
    return pltpu.CompilerParams(vmem_limit_bytes=VMEM_LIMIT)


def cost(flops, moved):
    return pl.CostEstimate(flops=flops, bytes_accessed=moved, transcendentals=0)


def wait_bytes(ref, sem):
    pltpu.make_async_copy(ref, ref, sem).wait()


def f32_dot(left, right):
    return jnp.dot(left, right, preferred_element_type=jnp.float32)


def pick_kernel(module_of, stored, out, sem):
    @pl.loop(0, out.shape[0], unroll=8)
    def _(path):
        pltpu.make_async_copy(stored.at[module_of[path]], out.at[path], sem).start()

    wait_bytes(out, sem)


def pick(module_of, stored):
    paths = module_of.shape[0]
    shape = (paths,) + stored.shape[1:]
    return pl.pallas_call(
        pick_kernel,
        out_shape=jax.ShapeDtypeStruct(shape, stored.dtype),
        in_specs=[SMEM, VMEM],
        out_specs=ANY,
        scratch_shapes=[pltpu.SemaphoreType.DMA],
        compiler_params=params(),
        cost_estimate=cost(0, 2 * math.prod(shape)),
        name="pick",
    )(module_of, stored)


def sigmoid(values):
    return 1.0 / (1.0 + jnp.exp(-values))


def starter(sems):
    def start(source, target, sem):
        copy = pltpu.make_async_copy(source, target, sems.at[sem])
        copy.start()
        return copy

    return start


def load_pair(start, shards_in, target, pair, sem):
    each = shards_in[0].shape[0]
    return [
        start(shards_in[i], target.at[pl.ds(i * each, each)], sem + i)
        for i in (2 * pair, 2 * pair + 1)
    ]


def send_rows(owner, delta, out, step, tile, sem):
    rows = out.shape[-2]

    @pl.loop(0, tile // rows, unroll=8)
    def _(inner):
        block = step * (tile // rows) + inner
        pltpu.make_async_copy(
            delta.at[:, pl.ds(pl.multiple_of(block * rows, rows), rows)],
            out.at[owner[block]],
            sem,
        ).start()


def first_kernel(scales, owner, arrived, order, grads_t, *refs):
    scale_in, scale_hid, rate = scales
    tok_in = refs[:4]
    out, weight, tok, grd_t, act, delta, sems = refs[4:]
    rows, cut = out.shape[2:]
    start = starter(sems)
    loads = [load_pair(start, tok_in, tok, 0, 3)]

    @pl.loop(0, arrived.shape[0], unroll=8)
    def _(block):
        pltpu.make_async_copy(
            arrived.at[owner[block], 0, :, pl.ds(0, cut)],
            weight.at[pl.ds(pl.multiple_of(block * rows, rows), rows)],
            sems.at[0],
        ).start()

    loads.append(load_pair(start, tok_in, tok, 1, 3))
    grads_copy = start(grads_t, grd_t, 2)
    wait_bytes(weight, sems.at[0])
    half = tok.shape[0] // 2
    for part in range(2):
        at = pl.ds(part * half, half)
        for copy in loads[part]:
            copy.wait()
        pre = f32_dot(tok[at, :], weight[...]) * scale_in
        act[at, :] = (pre * sigmoid(pre)).astype(jnp.bfloat16)
    grads_copy.wait()
    tile = 512

    @pl.loop(0, delta.shape[1] // tile)
    def _(step):
        at = pl.ds(pl.multiple_of(step * tile, tile), tile)
        grad = f32_dot(grd_t[at, :], act[...]) * scale_hid
        delta[0, at, :] = (grad * rate).astype(jnp.bfloat16)
        send_rows(owner, delta, out, step, tile, sems.at[1])

    wait_bytes(delta, sems.at[1])


def delta_first(scales, cut, owner, arrived, order, tokens, grads_t):
    paths, _, rows, _ = arrived.shape
    width, count = grads_t.shape
    bf16 = jnp.bfloat16
    return pl.pallas_call(
        functools.partial(first_kernel, scales),
        out_shape=jax.ShapeDtypeStruct((paths, 1, rows, cut), bf16),
        in_specs=[SMEM] + [ANY] * 7,
        out_specs=ANY,
        scratch_shapes=[
            pltpu.VMEM((width, cut), bf16),
            pltpu.VMEM((count, width), bf16),
            pltpu.VMEM((width, count), bf16),
            pltpu.VMEM((count, cut), bf16),
            pltpu.VMEM((1, width, cut), bf16),
            pltpu.SemaphoreType.DMA((7,)),
        ],
        compiler_params=params(),
        cost_estimate=cost(4 * count * width * cut, 4 * (count * width + width * cut)),
        name="delta_first",
    )(owner, arrived, order, grads_t, *tokens)


def rest_kernel(scales, owner, arrived, earlier, tokens_t, grads_t, *refs):
    scale_in, scale_hid, rate = scales
    tok_in, grd_in = refs[:4], refs[4:8]
    out, weight, tok, grd, tok_t, grd_t, act, slope, delta, sems = refs[8:]
    rows, cut = out.shape[2:]
    start = starter(sems)
    loads = [load_pair(start, tok_in, tok, 0, 4)]

    @pl.loop(0, arrived.shape[0], unroll=8)
    def _(block):
        pltpu.make_async_copy(
            arrived.at[owner[block]],
            weight.at[:, pl.ds(pl.multiple_of(block * rows, rows), rows)],
            sems.at[0],
        ).start()

    loads[0] += load_pair(start, grd_in, grd, 0, 8)
    wait_bytes(weight, sems.at[0])
    half = tok.shape[0] // 2
    for part in range(2):
        at = pl.ds(part * half, half)
        for copy in loads[part]:
            copy.wait()
        if part == 0:
            loads.append(load_pair(start, tok_in, tok, 1, 4) + load_pair(start, grd_in, grd, 1, 8))
            late = [start(grads_t, grd_t, 2), start(tokens_t, tok_t, 3)]
        pre = f32_dot(tok[at, :], weight[0]) * scale_in
        back = f32_dot(grd[at, :], weight[1]) * scale_hid
        sig = sigmoid(pre)
        act[at, :] = (pre[:, cut:] * sig[:, cut:]).astype(jnp.bfloat16)
        slope[at, :] = (back * (sig * (1.0 + pre * (1.0 - sig)))).astype(jnp.bfloat16)
    for copy in late:
        copy.wait()
    tile = 512

    @pl.loop(0, delta.shape[1] // tile)
    def _(step):
        at = pl.ds(pl.multiple_of(step * tile, tile), tile)
        grad_down = f32_dot(grd_t[at, :], act[...]) * scale_hid
        delta[0, at, :] = (grad_down * rate).astype(jnp.bfloat16)
        grad_up = f32_dot(tok_t[at, :], slope[...]) * scale_in
        up = (grad_up * rate).astype(jnp.bfloat16)
        delta[1, at, :] = up[:, :cut]
        delta[2, at, :] = up[:, cut:]
        send_rows(owner, delta, out, step, tile, sems.at[1])

    wait_bytes(delta, sems.at[1])


def delta_rest(scales, cut, owner, arrived, earlier, tokens, grads, tokens_t, grads_t):
    paths, halves, rows, cols = arrived.shape
    width, count = tokens_t.shape
    bf16 = jnp.bfloat16
    return pl.pallas_call(
        functools.partial(rest_kernel, scales),
        out_shape=jax.ShapeDtypeStruct((paths, 3, rows, cut), bf16),
        in_specs=[SMEM] + [ANY] * 12,
        out_specs=ANY,
        scratch_shapes=[
            pltpu.VMEM((halves, width, cols), bf16),
            pltpu.VMEM((count, width), bf16),
            pltpu.VMEM((count, width), bf16),
            pltpu.VMEM((width, count), bf16),
            pltpu.VMEM((width, count), bf16),
            pltpu.VMEM((count, cols - cut), bf16),
            pltpu.VMEM((count, cols), bf16),
            pltpu.VMEM((3, width, cut), bf16),
            pltpu.SemaphoreType.DMA((12,)),
        ],
        compiler_params=params(),
        cost_estimate=cost(7 * count * width * cols, 8 * (count * width + width * cols)),
        name="delta_rest",
    )(owner, arrived, earlier, tokens_t, grads_t, *tokens, *grads)


def outer_kernel(
    module_of, order, received_first, received, master, momentum, new_state, sending,
    got, mas, mom, state, updated, share, first, sems,
):
    modules, halves, rows, cols = state.shape
    step = outer_rate * (1.0 + outer_decay)
    cut = received.shape[3]
    low, high = pl.ds(0, cut), pl.ds(cut, cols - cut)
    loads = []
    for half in range(halves):
        pieces = ((received, 1, low), (received, 2, high))
        if half == 1:
            pieces = ((received_first, 0, low), (received, 0, high))
        pairs = [(source.at[:, slab], got.at[half, :, :, at]) for source, slab, at in pieces]
        pairs += [(master.at[:, half], mas.at[half]), (momentum.at[:, half], mom.at[half])]
        loads.append(
            [
                pltpu.make_async_copy(source, target, sems.at[4 * half + i])
                for i, (source, target) in enumerate(pairs)
            ]
        )
        for load in loads[half]:
            load.start()

    for module in range(modules + 1):
        first[module] = 0

    @pl.loop(0, module_of.shape[0], unroll=8)
    def _(path):
        first[module_of[path] + 1] += 1

    for module in range(modules):
        count = jnp.full(share.shape[1:], first[module + 1], jnp.int32)
        share[module] = 1.0 / count.astype(jnp.float32)
        first[module + 1] += first[module]

    for half in range(halves):
        for load in loads[half]:
            load.wait()

        @pl.loop(0, modules)
        def _(module):
            begin, end = first[module], first[module + 1]
            total = lax.fori_loop(
                begin,
                end,
                lambda i, acc: acc + got[half, order[i]].astype(jnp.float32),
                jnp.zeros((rows, cols), jnp.float32),
            )
            averaged = (total.reshape(-1, 8, cols) * share[module]).reshape(rows, cols)
            kept = outer_decay * mom[half, module]
            state[module, half] = kept + averaged
            weights = mas[half, module].astype(jnp.float32)
            updated[module, half] = (
                weights - (outer_rate * outer_decay) * kept - step * averaged
            ).astype(jnp.bfloat16)
            if half == halves - 1:
                pltpu.make_async_copy(
                    state.at[module], new_state.at[module], sems.at[8]
                ).start()

                @pl.loop(begin, end)
                def _(i):
                    pltpu.make_async_copy(
                        updated.at[module], sending.at[order[i]], sems.at[9]
                    ).start()

    wait_bytes(sending, sems.at[9])
    wait_bytes(state, sems.at[8])


def outer(module_of, order, received_first, received, master, momentum):
    paths = received.shape[0]
    modules, halves, rows, cols = master.shape
    f32, bf16 = jnp.float32, jnp.bfloat16
    return pl.pallas_call(
        outer_kernel,
        out_shape=(
            jax.ShapeDtypeStruct(momentum.shape, f32),
            jax.ShapeDtypeStruct((paths, halves, rows, cols), bf16),
        ),
        in_specs=[SMEM, SMEM, ANY, ANY, ANY, ANY],
        out_specs=(ANY, ANY),
        scratch_shapes=[
            pltpu.VMEM((halves, paths, rows, cols), bf16),
            pltpu.VMEM((halves, modules, rows, cols), bf16),
            pltpu.VMEM((halves, modules, rows, cols), f32),
            pltpu.VMEM(momentum.shape, f32),
            pltpu.VMEM(master.shape, bf16),
            pltpu.VMEM((modules, 8, cols), f32),
            pltpu.SMEM((modules + 1,), jnp.int32),
            pltpu.SemaphoreType.DMA((10,)),
        ],
        compiler_params=params(),
        cost_estimate=cost(2 * paths * rows * cols, 8 * paths * rows * cols),
        name="outer",
    )(module_of, order, received_first, received, master, momentum)


def home_kernel(groups, owner, back, out, buf, place, sems):
    per = back.shape[0] // groups
    loads = []
    for group in range(groups):
        part = pl.ds(group * per, per)
        loads.append(
            pltpu.make_async_copy(back.at[part], buf.at[part], sems.at[group])
        )
        loads[-1].start()

    @pl.loop(0, back.shape[0], unroll=8)
    def _(block):
        place[owner[block]] = block

    for group in range(groups):
        loads[group].wait()

        @pl.loop(0, per, unroll=8)
        def _(inner):
            holder = group * per + inner
            pltpu.make_async_copy(
                buf.at[holder], out.at[:, place[holder]], sems.at[groups]
            ).start()

    wait_bytes(buf, sems.at[groups])


def bring_home(owner, back):
    paths, halves, rows, cols = back.shape
    groups = 4
    return pl.pallas_call(
        functools.partial(home_kernel, groups),
        out_shape=jax.ShapeDtypeStruct((halves, paths, rows, cols), back.dtype),
        in_specs=[SMEM, ANY],
        out_specs=ANY,
        scratch_shapes=[
            pltpu.VMEM(back.shape, back.dtype),
            pltpu.SMEM((paths,), jnp.int32),
            pltpu.SemaphoreType.DMA((groups + 1,)),
        ],
        compiler_params=params(),
        cost_estimate=cost(0, 4 * paths * halves * rows * cols),
        name="bring_home",
    )(owner, back)


def collect(tokens, grads):
    count = lax.axis_size("fsdp")
    right = [(i, (i + 1) % count) for i in range(count)]
    left = [(i, (i - 1) % count) for i in range(count)]
    tok_left = lax.ppermute(tokens, "fsdp", right)
    grd_right = lax.ppermute(grads, "fsdp", left)
    grd_left = lax.ppermute(grads, "fsdp", right)
    tok_right = lax.ppermute(tokens, "fsdp", left)
    grd_far = lax.ppermute(grd_right, "fsdp", left)
    tok_far = lax.ppermute(tok_left, "fsdp", right)
    return (tokens, tok_left, tok_right, tok_far), (grads, grd_left, grd_right, grd_far)


def exchange(blocks):
    return lax.all_to_all(blocks, "path", split_axis=0, concat_axis=0, tiled=True)


def shards(inputs, cotangent, master, momentum, sharing, block_owner):
    block_cols = master.shape[3]
    module_of = sharing[:, 0]
    order = jnp.argsort(module_of)
    fsdp = lax.axis_size("fsdp")
    rows, model_width = inputs.shape
    fill = ((0, -rows % 64), (0, 0))
    tokens, grads = collect(
        *lax.optimization_barrier((jnp.pad(inputs, fill), jnp.pad(cotangent, fill)))
    )
    tokens_t, grads_t = jnp.concatenate(tokens).T, jnp.concatenate(grads).T
    scales = (
        1.0 / math.sqrt(model_width),
        1.0 / math.sqrt(block_cols * fsdp),
        inner_rate / math.sqrt(rows * fsdp),
    )
    arrived = exchange(pick(module_of, master))
    cut = block_cols // 2
    begun = delta_first(scales, cut, block_owner, arrived, order, tokens, grads_t)
    rest = delta_rest(
        scales, cut, block_owner, arrived, begun, tokens, grads, tokens_t, grads_t
    )
    got_first, got = exchange(begun), exchange(rest)
    new_state, sending = outer(module_of, order, got_first, got, master, momentum)
    own_module = bring_home(block_owner, exchange(sending))
    return (new_state, own_module.reshape(1, 2, model_width, block_cols))


def solution(mesh):
    placed = (
        P(("path", "fsdp"), None),
        P(("path", "fsdp"), None),
        P(None, None, "path", "fsdp"),
        P(None, None, "path", "fsdp"),
        P(),
        P(),
    )
    return jax.shard_map(
        shards,
        mesh=mesh,
        in_specs=placed,
        out_specs=(P(None, None, "path", "fsdp"), P("path", None, None, "fsdp")),
        check_vma=False,
    )
```

```python
import functools
import math

import jax
import jax.numpy as jnp
from jax import lax
from jax.experimental import pallas as pl
from jax.experimental.pallas import tpu as pltpu
from jax.sharding import PartitionSpec as P

inner_rate = 10.0
outer_rate = 0.7
outer_decay = 0.9

VMEM_LIMIT = 56 * 1024 * 1024
ANY = pl.BlockSpec(memory_space=pl.ANY)
SMEM = pl.BlockSpec(memory_space=pltpu.SMEM)
VMEM = pl.BlockSpec(memory_space=pltpu.VMEM)


def params():
    return pltpu.CompilerParams(vmem_limit_bytes=VMEM_LIMIT)


def cost(flops, moved):
    return pl.CostEstimate(flops=flops, bytes_accessed=moved, transcendentals=0)


def wait_bytes(ref, sem):
    pltpu.make_async_copy(ref, ref, sem).wait()


def f32_dot(left, right):
    return jnp.dot(left, right, preferred_element_type=jnp.float32)


def pick_kernel(module_of, stored, out, sem):
    @pl.loop(0, out.shape[0], unroll=8)
    def _(path):
        pltpu.make_async_copy(stored.at[module_of[path]], out.at[path], sem).start()

    wait_bytes(out, sem)


def pick(module_of, stored):
    paths = module_of.shape[0]
    shape = (paths,) + stored.shape[1:]
    return pl.pallas_call(
        pick_kernel,
        out_shape=jax.ShapeDtypeStruct(shape, stored.dtype),
        in_specs=[SMEM, VMEM],
        out_specs=ANY,
        scratch_shapes=[pltpu.SemaphoreType.DMA],
        compiler_params=params(),
        cost_estimate=cost(0, 2 * math.prod(shape)),
        name="pick",
    )(module_of, stored)


def sigmoid(values):
    return 1.0 / (1.0 + jnp.exp(-values))


def delta_kernel(scales, tiles, owner, arrived, order, base, tokens_t, grads_t, *refs):
    scale_in, scale_hid, rate = scales
    tile_cols, tile_rows = tiles
    tok_in, grd_in = refs[:4], refs[4:8]
    out, weight, tok, grd, tok_t, grd_t, act, slope, delta, sems = refs[8:]
    rows = arrived.shape[2]
    each = tok_in[0].shape[0]

    def start(source, target, sem):
        copy = pltpu.make_async_copy(source, target, sems.at[sem])
        copy.start()
        return copy

    def load(shards_in, target, i, sem):
        return start(shards_in[i], target.at[pl.ds(i * each, each)], sem + i)

    loads = [[load(tok_in, tok, 0, 4), load(tok_in, tok, 1, 4)]]

    @pl.loop(0, arrived.shape[0], unroll=8)
    def _(block):
        pltpu.make_async_copy(
            arrived.at[owner[block]],
            weight.at[:, pl.ds(pl.multiple_of(block * rows, rows), rows)],
            sems.at[0],
        ).start()

    loads[0] += [load(grd_in, grd, 0, 8), load(grd_in, grd, 1, 8)]
    wait_bytes(weight, sems.at[0])
    for part in range(2):
        at = pl.ds(part * 2 * each, 2 * each)
        for copy in loads[part]:
            copy.wait()
        if part == 0:
            loads.append([load(tok_in, tok, i, 4) for i in (2, 3)])
            loads[1] += [load(grd_in, grd, i, 8) for i in (2, 3)]
            late = [start(grads_t, grd_t, 2), start(tokens_t, tok_t, 3)]

        @pl.loop(0, act.shape[1] // tile_cols)
        def _(step):
            cols = pl.ds(pl.multiple_of(step * tile_cols, tile_cols), tile_cols)
            pre = f32_dot(tok[at, :], weight[0, :, cols]) * scale_in
            back = f32_dot(grd[at, :], weight[1, :, cols]) * scale_hid
            sig = sigmoid(pre)
            act[at, cols] = (pre * sig).astype(jnp.bfloat16)
            slope[at, cols] = (back * (sig * (1.0 + pre * (1.0 - sig)))).astype(jnp.bfloat16)

    for copy in late:
        copy.wait()

    @pl.loop(0, delta.shape[1] // tile_rows)
    def _(step):
        at = pl.ds(pl.multiple_of(step * tile_rows, tile_rows), tile_rows)
        grad_down = f32_dot(grd_t[at, :], act[...]) * scale_hid
        delta[1, at, :] = (grad_down * rate).astype(jnp.bfloat16)
        grad_up = f32_dot(tok_t[at, :], slope[...]) * scale_in
        delta[0, at, :] = (grad_up * rate).astype(jnp.bfloat16)

        @pl.loop(0, tile_rows // rows, unroll=8)
        def _(inner):
            block = step * (tile_rows // rows) + inner
            pltpu.make_async_copy(
                delta.at[:, pl.ds(pl.multiple_of(block * rows, rows), rows)],
                out.at[owner[block]],
                sems.at[1],
            ).start()

    wait_bytes(delta, sems.at[1])


def path_delta(scales, owner, arrived, order, base, tokens, grads, tokens_t, grads_t):
    _, halves, _, cols = arrived.shape
    width, count = tokens_t.shape
    bf16 = jnp.bfloat16
    return pl.pallas_call(
        functools.partial(delta_kernel, scales, (1024, 512)),
        out_shape=jax.ShapeDtypeStruct(arrived.shape, bf16),
        in_specs=[SMEM] + [ANY] * 13,
        out_specs=ANY,
        scratch_shapes=[
            pltpu.VMEM((halves, width, cols), bf16),
            pltpu.VMEM((count, width), bf16),
            pltpu.VMEM((count, width), bf16),
            pltpu.VMEM((width, count), bf16),
            pltpu.VMEM((width, count), bf16),
            pltpu.VMEM((count, cols), bf16),
            pltpu.VMEM((count, cols), bf16),
            pltpu.VMEM((halves, width, cols), bf16),
            pltpu.SemaphoreType.DMA((12,)),
        ],
        compiler_params=params(),
        cost_estimate=cost(8 * count * width * cols, 8 * (count * width + width * cols)),
        name="path_delta",
    )(owner, arrived, order, base, tokens_t, grads_t, *tokens, *grads)


def begin_of(module_of, first, share):
    modules = share.shape[0]
    for module in range(modules + 1):
        first[module] = 0

    @pl.loop(0, module_of.shape[0], unroll=8)
    def _(path):
        first[module_of[path] + 1] += 1

    for module in range(modules):
        count = jnp.full(share.shape[1:], first[module + 1], jnp.int32)
        share[module] = 1.0 / count.astype(jnp.float32)
        first[module + 1] += first[module]


def load_halves(sources, targets, sems):
    loads = []
    for half in range(2):
        loads.append([])
        for source, target in zip(sources, targets, strict=True):
            sem = sems.at[half * len(sources) + len(loads[half])]
            loads[half].append(pltpu.make_async_copy(source.at[:, half], target.at[half], sem))
            loads[half][-1].start()
    return loads


def average_of(half, module, order, got, first, share):
    rows, cols = got.shape[2:]
    total = lax.fori_loop(
        first[module],
        first[module + 1],
        lambda i, acc: acc + got[half, order[i]].astype(jnp.float32),
        jnp.zeros((rows, cols), jnp.float32),
    )
    return (total.reshape(-1, 8, cols) * share[module]).reshape(rows, cols)


def update_kernel(
    module_of, order, received, base_in, sending, first, got, base, updated, share, sems
):
    modules, halves = updated.shape[:2]
    step = outer_rate * (1.0 + outer_decay)
    loads = load_halves((received, base_in), (got, base), sems)
    begin_of(module_of, first, share)
    for half in range(halves):
        for load in loads[half]:
            load.wait()

        @pl.loop(0, modules)
        def _(module):
            averaged = average_of(half, module, order, got, first, share)
            updated[module, half] = (base[half, module] - step * averaged).astype(jnp.bfloat16)
            if half == halves - 1:

                @pl.loop(first[module], first[module + 1])
                def _(i):
                    pltpu.make_async_copy(
                        updated.at[module], sending.at[order[i]], sems.at[4]
                    ).start()

    wait_bytes(sending, sems.at[4])


def update(module_of, order, received, base):
    paths, halves, rows, cols = received.shape
    modules = base.shape[0]
    f32, bf16 = jnp.float32, jnp.bfloat16
    return pl.pallas_call(
        update_kernel,
        out_shape=(
            jax.ShapeDtypeStruct(received.shape, bf16),
            jax.ShapeDtypeStruct((modules + 1,), jnp.int32),
        ),
        in_specs=[SMEM, SMEM, ANY, ANY],
        out_specs=(ANY, SMEM),
        scratch_shapes=[
            pltpu.VMEM((halves, paths, rows, cols), bf16),
            pltpu.VMEM((halves, modules, rows, cols), f32),
            pltpu.VMEM(base.shape, bf16),
            pltpu.VMEM((modules, 8, cols), f32),
            pltpu.SemaphoreType.DMA((5,)),
        ],
        compiler_params=params(),
        cost_estimate=cost(2 * paths * rows * cols, 8 * paths * rows * cols),
        name="update",
    )(module_of, order, received, base)


def state_kernel(
    first, order, received, momentum, new_state, got, mom, state, share, sems
):
    modules, halves = state.shape[:2]
    loads = load_halves((received, momentum), (got, mom), sems)
    for module in range(modules):
        count = jnp.full(share.shape[1:], first[module + 1] - first[module], jnp.int32)
        share[module] = 1.0 / count.astype(jnp.float32)
    for half in range(halves):
        for load in loads[half]:
            load.wait()

        @pl.loop(0, modules)
        def _(module):
            averaged = average_of(half, module, order, got, first, share)
            state[module, half] = outer_decay * mom[half, module] + averaged

    store = pltpu.make_async_copy(state, new_state, sems.at[4])
    store.start()
    store.wait()


def next_state(first, order, received, momentum):
    paths, halves, rows, cols = received.shape
    modules = momentum.shape[0]
    f32, bf16 = jnp.float32, jnp.bfloat16
    return pl.pallas_call(
        state_kernel,
        out_shape=jax.ShapeDtypeStruct(momentum.shape, f32),
        in_specs=[SMEM, SMEM, ANY, ANY],
        out_specs=ANY,
        scratch_shapes=[
            pltpu.VMEM((halves, paths, rows, cols), bf16),
            pltpu.VMEM((halves, modules, rows, cols), f32),
            pltpu.VMEM(momentum.shape, f32),
            pltpu.VMEM((modules, 8, cols), f32),
            pltpu.SemaphoreType.DMA((5,)),
        ],
        compiler_params=params(),
        cost_estimate=cost(2 * paths * rows * cols, 8 * paths * rows * cols),
        name="next_state",
    )(first, order, received, momentum)


def home_kernel(groups, owner, back, out, buf, place, sems):
    per = back.shape[0] // groups
    loads = []
    for group in range(groups):
        part = pl.ds(group * per, per)
        loads.append(
            pltpu.make_async_copy(back.at[part], buf.at[part], sems.at[group])
        )
        loads[-1].start()

    @pl.loop(0, back.shape[0], unroll=8)
    def _(block):
        place[owner[block]] = block

    for group in range(groups):
        loads[group].wait()

        @pl.loop(0, per, unroll=8)
        def _(inner):
            holder = group * per + inner
            pltpu.make_async_copy(
                buf.at[holder], out.at[:, place[holder]], sems.at[groups]
            ).start()

    wait_bytes(buf, sems.at[groups])


def bring_home(owner, back):
    paths, halves, rows, cols = back.shape
    groups = 4
    return pl.pallas_call(
        functools.partial(home_kernel, groups),
        out_shape=jax.ShapeDtypeStruct((halves, paths, rows, cols), back.dtype),
        in_specs=[SMEM, ANY],
        out_specs=ANY,
        scratch_shapes=[
            pltpu.VMEM(back.shape, back.dtype),
            pltpu.SMEM((paths,), jnp.int32),
            pltpu.SemaphoreType.DMA((groups + 1,)),
        ],
        compiler_params=params(),
        cost_estimate=cost(0, 4 * paths * halves * rows * cols),
        name="bring_home",
    )(owner, back)


def collect(tokens, grads):
    count = lax.axis_size("fsdp")
    right = [(i, (i + 1) % count) for i in range(count)]
    left = [(i, (i - 1) % count) for i in range(count)]
    tok_left = lax.ppermute(tokens, "fsdp", right)
    grd_right = lax.ppermute(grads, "fsdp", left)
    grd_left = lax.ppermute(grads, "fsdp", right)
    tok_right = lax.ppermute(tokens, "fsdp", left)
    grd_far = lax.ppermute(grd_right, "fsdp", left)
    tok_far = lax.ppermute(tok_left, "fsdp", right)
    return (tokens, tok_left, tok_right, tok_far), (grads, grd_left, grd_right, grd_far)


def exchange(blocks):
    return lax.all_to_all(blocks, "path", split_axis=0, concat_axis=0, tiled=True)


def shards(inputs, cotangent, master, momentum, sharing, block_owner):
    block_cols = master.shape[3]
    module_of = sharing[:, 0]
    order = jnp.argsort(module_of)
    fsdp = lax.axis_size("fsdp")
    rows, model_width = inputs.shape
    fill = ((0, -rows % 64), (0, 0))
    tokens, grads = collect(
        *lax.optimization_barrier((jnp.pad(inputs, fill), jnp.pad(cotangent, fill)))
    )
    tokens_t, grads_t = jnp.concatenate(tokens).T, jnp.concatenate(grads).T
    scales = (
        1.0 / math.sqrt(model_width),
        1.0 / math.sqrt(block_cols * fsdp),
        inner_rate / math.sqrt(rows * fsdp),
    )
    arrived = exchange(pick(module_of, master))
    base = master.astype(jnp.float32) - (outer_rate * outer_decay * outer_decay) * momentum
    delta = path_delta(
        scales, block_owner, arrived, order, base, tokens, grads, tokens_t, grads_t
    )
    received = exchange(delta)
    sending, first = update(module_of, order, received, base)
    new_state = next_state(first, order, received, momentum)
    own_module = bring_home(block_owner, exchange(sending))
    return (new_state, own_module.reshape(1, 2, model_width, block_cols))


def solution(mesh):
    placed = (
        P(("path", "fsdp"), None),
        P(("path", "fsdp"), None),
        P(None, None, "path", "fsdp"),
        P(None, None, "path", "fsdp"),
        P(),
        P(),
    )
    return jax.shard_map(
        shards,
        mesh=mesh,
        in_specs=placed,
        out_specs=(P(None, None, "path", "fsdp"), P("path", None, None, "fsdp")),
        check_vma=False,
    )
```

```python
import functools
import math

import jax
import jax.numpy as jnp
from jax import lax
from jax.experimental import pallas as pl
from jax.experimental.pallas import tpu as pltpu
from jax.sharding import PartitionSpec as P

inner_rate = 10.0
outer_rate = 0.7
outer_decay = 0.9

VMEM_LIMIT = 56 * 1024 * 1024
ANY = pl.BlockSpec(memory_space=pl.ANY)
SMEM = pl.BlockSpec(memory_space=pltpu.SMEM)
VMEM = pl.BlockSpec(memory_space=pltpu.VMEM)


def params():
    return pltpu.CompilerParams(vmem_limit_bytes=VMEM_LIMIT)


def cost(flops, moved):
    return pl.CostEstimate(flops=flops, bytes_accessed=moved, transcendentals=0)


def wait_bytes(ref, sem):
    pltpu.make_async_copy(ref, ref, sem).wait()


def f32_dot(left, right):
    return jnp.dot(left, right, preferred_element_type=jnp.float32)


def pick_kernel(module_of, stored, out, sem):
    @pl.loop(0, out.shape[0], unroll=8)
    def _(path):
        pltpu.make_async_copy(stored.at[module_of[path]], out.at[path], sem).start()

    wait_bytes(out, sem)


def pick(module_of, stored):
    paths = module_of.shape[0]
    shape = (paths,) + stored.shape[1:]
    return pl.pallas_call(
        pick_kernel,
        out_shape=jax.ShapeDtypeStruct(shape, stored.dtype),
        in_specs=[SMEM, VMEM],
        out_specs=ANY,
        scratch_shapes=[pltpu.SemaphoreType.DMA],
        compiler_params=params(),
        cost_estimate=cost(0, 2 * math.prod(shape)),
        name="pick",
    )(module_of, stored)


def sigmoid(values):
    return 1.0 / (1.0 + jnp.exp(-values))


def delta_kernel(scales, tiles, owner, arrived, order, base, tokens_t, grads_t, *refs):
    scale_in, scale_hid, rate = scales
    tile_cols, tile_rows = tiles
    tok_in, grd_in = refs[:4], refs[4:8]
    out, weight, tok, grd, tok_t, grd_t, act, slope, delta, sems = refs[8:]
    rows = arrived.shape[2]
    each = tok_in[0].shape[0]

    def start(source, target, sem):
        copy = pltpu.make_async_copy(source, target, sems.at[sem])
        copy.start()
        return copy

    def load(shards_in, target, i, sem):
        return start(shards_in[i], target.at[pl.ds(i * each, each)], sem + i)

    loads = [[load(tok_in, tok, 0, 4), load(tok_in, tok, 1, 4)]]

    @pl.loop(0, arrived.shape[0], unroll=8)
    def _(block):
        pltpu.make_async_copy(
            arrived.at[owner[block]],
            weight.at[:, pl.ds(pl.multiple_of(block * rows, rows), rows)],
            sems.at[0],
        ).start()

    loads[0] += [load(grd_in, grd, 0, 8), load(grd_in, grd, 1, 8)]
    wait_bytes(weight, sems.at[0])
    for part in range(2):
        at = pl.ds(part * 2 * each, 2 * each)
        for copy in loads[part]:
            copy.wait()
        if part == 0:
            loads.append([load(tok_in, tok, i, 4) for i in (2, 3)])
            loads[1] += [load(grd_in, grd, i, 8) for i in (2, 3)]
            late = [start(grads_t, grd_t, 2), start(tokens_t, tok_t, 3)]

        @pl.loop(0, act.shape[1] // tile_cols)
        def _(step):
            cols = pl.ds(pl.multiple_of(step * tile_cols, tile_cols), tile_cols)
            pre = f32_dot(tok[at, :], weight[0, :, cols]) * scale_in
            back = f32_dot(grd[at, :], weight[1, :, cols]) * scale_hid
            sig = sigmoid(pre)
            act[at, cols] = (pre * sig).astype(jnp.bfloat16)
            slope[at, cols] = (back * (sig * (1.0 + pre * (1.0 - sig)))).astype(jnp.bfloat16)

    for copy in late:
        copy.wait()

    @pl.loop(0, delta.shape[1] // tile_rows)
    def _(step):
        at = pl.ds(pl.multiple_of(step * tile_rows, tile_rows), tile_rows)
        grad_down = f32_dot(grd_t[at, :], act[...]) * scale_hid
        delta[1, at, :] = (grad_down * rate).astype(jnp.bfloat16)
        grad_up = f32_dot(tok_t[at, :], slope[...]) * scale_in
        delta[0, at, :] = (grad_up * rate).astype(jnp.bfloat16)

        @pl.loop(0, tile_rows // rows, unroll=8)
        def _(inner):
            block = step * (tile_rows // rows) + inner
            pltpu.make_async_copy(
                delta.at[:, pl.ds(pl.multiple_of(block * rows, rows), rows)],
                out.at[owner[block]],
                sems.at[1],
            ).start()

    wait_bytes(delta, sems.at[1])


def path_delta(scales, owner, arrived, order, base, tokens, grads, tokens_t, grads_t):
    _, halves, _, cols = arrived.shape
    width, count = tokens_t.shape
    bf16 = jnp.bfloat16
    return pl.pallas_call(
        functools.partial(delta_kernel, scales, (1024, 512)),
        out_shape=jax.ShapeDtypeStruct(arrived.shape, bf16),
        in_specs=[SMEM] + [ANY] * 13,
        out_specs=ANY,
        scratch_shapes=[
            pltpu.VMEM((halves, width, cols), bf16),
            pltpu.VMEM((count, width), bf16),
            pltpu.VMEM((count, width), bf16),
            pltpu.VMEM((width, count), bf16),
            pltpu.VMEM((width, count), bf16),
            pltpu.VMEM((count, cols), bf16),
            pltpu.VMEM((count, cols), bf16),
            pltpu.VMEM((halves, width, cols), bf16),
            pltpu.SemaphoreType.DMA((12,)),
        ],
        compiler_params=params(),
        cost_estimate=cost(8 * count * width * cols, 8 * (count * width + width * cols)),
        name="path_delta",
    )(owner, arrived, order, base, tokens_t, grads_t, *tokens, *grads)


def begin_of(module_of, first, share):
    modules = share.shape[0]
    for module in range(modules + 1):
        first[module] = 0

    @pl.loop(0, module_of.shape[0], unroll=8)
    def _(path):
        first[module_of[path] + 1] += 1

    for module in range(modules):
        count = jnp.full(share.shape[1:], first[module + 1], jnp.int32)
        share[module] = 1.0 / count.astype(jnp.float32)
        first[module + 1] += first[module]


def load_halves(sources, targets, sems):
    loads = []
    for half in range(2):
        loads.append([])
        for source, target in zip(sources, targets, strict=True):
            sem = sems.at[half * len(sources) + len(loads[half])]
            loads[half].append(pltpu.make_async_copy(source.at[:, half], target.at[half], sem))
            loads[half][-1].start()
    return loads


def average_of(half, module, order, got, first, share):
    rows, cols = got.shape[2:]
    total = lax.fori_loop(
        first[module],
        first[module + 1],
        lambda i, acc: acc + got[half, order[i]].astype(jnp.float32),
        jnp.zeros((rows, cols), jnp.float32),
    )
    return (total.reshape(-1, 8, cols) * share[module]).reshape(rows, cols)


def update_kernel(
    module_of, order, received, base_in, sending, first, got, base, updated, share, sems
):
    modules, halves = updated.shape[:2]
    step = outer_rate * (1.0 + outer_decay)
    loads = load_halves((received, base_in), (got, base), sems)
    begin_of(module_of, first, share)
    for half in range(halves):
        for load in loads[half]:
            load.wait()

        @pl.loop(0, modules)
        def _(module):
            averaged = average_of(half, module, order, got, first, share)
            updated[module, half] = (base[half, module] - step * averaged).astype(jnp.bfloat16)
            if half == halves - 1:

                @pl.loop(first[module], first[module + 1])
                def _(i):
                    pltpu.make_async_copy(
                        updated.at[module], sending.at[order[i]], sems.at[4]
                    ).start()

    wait_bytes(sending, sems.at[4])


def update(module_of, order, received, base):
    paths, halves, rows, cols = received.shape
    modules = base.shape[0]
    f32, bf16 = jnp.float32, jnp.bfloat16
    return pl.pallas_call(
        update_kernel,
        out_shape=(
            jax.ShapeDtypeStruct(received.shape, bf16),
            jax.ShapeDtypeStruct((modules + 1,), jnp.int32),
        ),
        in_specs=[SMEM, SMEM, ANY, ANY],
        out_specs=(ANY, SMEM),
        scratch_shapes=[
            pltpu.VMEM((halves, paths, rows, cols), bf16),
            pltpu.VMEM((halves, modules, rows, cols), f32),
            pltpu.VMEM(base.shape, bf16),
            pltpu.VMEM((modules, 8, cols), f32),
            pltpu.SemaphoreType.DMA((5,)),
        ],
        compiler_params=params(),
        cost_estimate=cost(2 * paths * rows * cols, 8 * paths * rows * cols),
        name="update",
    )(module_of, order, received, base)


def state_kernel(
    first, order, received, momentum, new_state, got, mom, state, share, sems
):
    modules, halves = state.shape[:2]
    loads = load_halves((received, momentum), (got, mom), sems)
    for module in range(modules):
        count = jnp.full(share.shape[1:], first[module + 1] - first[module], jnp.int32)
        share[module] = 1.0 / count.astype(jnp.float32)
    for half in range(halves):
        for load in loads[half]:
            load.wait()

        @pl.loop(0, modules)
        def _(module):
            averaged = average_of(half, module, order, got, first, share)
            state[module, half] = outer_decay * mom[half, module] + averaged

    store = pltpu.make_async_copy(state, new_state, sems.at[4])
    store.start()
    store.wait()


def next_state(first, order, received, momentum):
    paths, halves, rows, cols = received.shape
    modules = momentum.shape[0]
    f32, bf16 = jnp.float32, jnp.bfloat16
    return pl.pallas_call(
        state_kernel,
        out_shape=jax.ShapeDtypeStruct(momentum.shape, f32),
        in_specs=[SMEM, SMEM, ANY, ANY],
        out_specs=ANY,
        scratch_shapes=[
            pltpu.VMEM((halves, paths, rows, cols), bf16),
            pltpu.VMEM((halves, modules, rows, cols), f32),
            pltpu.VMEM(momentum.shape, f32),
            pltpu.VMEM((modules, 8, cols), f32),
            pltpu.SemaphoreType.DMA((5,)),
        ],
        compiler_params=params(),
        cost_estimate=cost(2 * paths * rows * cols, 8 * paths * rows * cols),
        name="next_state",
    )(first, order, received, momentum)


def home_kernel(groups, owner, back, out, buf, place, sems):
    per = back.shape[0] // groups
    loads = []
    for group in range(groups):
        part = pl.ds(group * per, per)
        loads.append(
            pltpu.make_async_copy(back.at[part], buf.at[part], sems.at[group])
        )
        loads[-1].start()

    @pl.loop(0, back.shape[0], unroll=8)
    def _(block):
        place[owner[block]] = block

    for group in range(groups):
        loads[group].wait()

        @pl.loop(0, per, unroll=8)
        def _(inner):
            holder = group * per + inner
            pltpu.make_async_copy(
                buf.at[holder], out.at[:, place[holder]], sems.at[groups]
            ).start()

    wait_bytes(buf, sems.at[groups])


def bring_home(owner, back):
    paths, halves, rows, cols = back.shape
    groups = 8
    return pl.pallas_call(
        functools.partial(home_kernel, groups),
        out_shape=jax.ShapeDtypeStruct((halves, paths, rows, cols), back.dtype),
        in_specs=[SMEM, ANY],
        out_specs=ANY,
        scratch_shapes=[
            pltpu.VMEM(back.shape, back.dtype),
            pltpu.SMEM((paths,), jnp.int32),
            pltpu.SemaphoreType.DMA((groups + 1,)),
        ],
        compiler_params=params(),
        cost_estimate=cost(0, 4 * paths * halves * rows * cols),
        name="bring_home",
    )(owner, back)


def collect(tokens, grads):
    count = lax.axis_size("fsdp")
    right = [(i, (i + 1) % count) for i in range(count)]
    left = [(i, (i - 1) % count) for i in range(count)]
    tok_left = lax.ppermute(tokens, "fsdp", right)
    grd_right = lax.ppermute(grads, "fsdp", left)
    grd_left = lax.ppermute(grads, "fsdp", right)
    tok_right = lax.ppermute(tokens, "fsdp", left)
    grd_far = lax.ppermute(grd_right, "fsdp", left)
    tok_far = lax.ppermute(tok_left, "fsdp", right)
    return (tokens, tok_left, tok_right, tok_far), (grads, grd_left, grd_right, grd_far)


def exchange(blocks):
    return lax.all_to_all(blocks, "path", split_axis=0, concat_axis=0, tiled=True)


def shards(inputs, cotangent, master, momentum, sharing, block_owner):
    block_cols = master.shape[3]
    module_of = sharing[:, 0]
    order = jnp.argsort(module_of)
    fsdp = lax.axis_size("fsdp")
    rows, model_width = inputs.shape
    fill = ((0, -rows % 64), (0, 0))
    tokens, grads = collect(
        *lax.optimization_barrier((jnp.pad(inputs, fill), jnp.pad(cotangent, fill)))
    )
    tokens_t, grads_t = jnp.concatenate(tokens).T, jnp.concatenate(grads).T
    scales = (
        1.0 / math.sqrt(model_width),
        1.0 / math.sqrt(block_cols * fsdp),
        inner_rate / math.sqrt(rows * fsdp),
    )
    arrived = exchange(pick(module_of, master))
    base = master.astype(jnp.float32) - (outer_rate * outer_decay * outer_decay) * momentum
    delta = path_delta(
        scales, block_owner, arrived, order, base, tokens, grads, tokens_t, grads_t
    )
    received = exchange(delta)
    sending, first = update(module_of, order, received, base)
    new_state = next_state(first, order, received, momentum)
    own_module = bring_home(block_owner, exchange(sending))
    return (new_state, own_module.reshape(1, 2, model_width, block_cols))


def solution(mesh):
    placed = (
        P(("path", "fsdp"), None),
        P(("path", "fsdp"), None),
        P(None, None, "path", "fsdp"),
        P(None, None, "path", "fsdp"),
        P(),
        P(),
    )
    return jax.shard_map(
        shards,
        mesh=mesh,
        in_specs=placed,
        out_specs=(P(None, None, "path", "fsdp"), P("path", None, None, "fsdp")),
        check_vma=False,
    )
```
